256 devices in a mesh: dp: 32 (over y, x, core), fsdp: 8 (over z).
Axes of the slice: x: 4, y: 4, z: 8, core: 2. Of those that a mesh axis runs over, the one named last changes fastest.
Arguments:
- queries: bfloat16 [32768, 2048], P(('dp', 'fsdp')), may hold values from -24 to 24
- inputs: bfloat16 [32768, 2048], P(('dp', 'fsdp')), may hold values from -24 to 24
- key_weight: bfloat16 [2048, 512], P('fsdp'), may hold values from -0.125 to 0.125
- value_weight: bfloat16 [2048, 512], P('fsdp'), may hold values from -0.125 to 0.125
- lengths: int32 [256, 8], P(('dp', 'fsdp')), may hold values from 1 to 24, 128 in all within a row
- doc_ranks: int32 [256, 8], P(('dp', 'fsdp')), may hold values from 0 to 31, as said below
- cotangent: bfloat16 [196608, 2048], P(('dp', 'fsdp')), may hold values from -6 to 6
Outputs:
- d_queries: bfloat16 [32768, 2048], P(('dp', 'fsdp'))
- d_inputs: bfloat16 [32768, 2048], P(('dp', 'fsdp'))
- d_key_weight: float32 [2048, 512], P(('dp', 'fsdp'))
- d_value_weight: float32 [2048, 512], P(('dp', 'fsdp'))
The draws below stay inside these ranges and needn't reach their ends.
Inputs may be any that keep to these rules, and one draw needn't show every extreme that they name: Row m lists the lengths of the 8 documents packed in order into the 128 tokens of micro-batch m; they sum to 128. Row m names 8 different data ranks: document k of micro-batch m = i * 8 + j goes to slot i of data rank doc_ranks[m, k] at the same fsdp index; slots that no document reaches stay empty.
All inputs are finite; a program needn't handle non-finite values.
Results may differ from the reference program's by a relative error of at most 0.02.
Values may be sent and summed in bfloat16 or wider, within the bound.
A program may use at most 128 MiB of HBM per device.

```python
import math
import jax
import jax.numpy as jnp
import numpy as np
from jax import lax

D_WIN = 2048
HEAD_DIM = 128
ROWS = 128
DOCS = 8
Q_WIDTH = 2048
KV_WIDTH = 512
SLOT = 24
BUFFER = 768
TOKENS = 32768
N_DP = 32
N_FSDP = 8


def draw_queries(key, part):
    key = jax.random.fold_in(key, 17)
    normal_part = jnp.clip(jax.random.normal(key, (TOKENS, Q_WIDTH), jnp.float32), -4.0, 4.0)
    return normal_part.astype(jnp.bfloat16)


def draw_doc_ranks(key, part):
    key = jax.random.fold_in(key, 29)
    random_bits = jax.random.randint(key, (N_DP * N_FSDP, N_DP), 0, 1 << 20, dtype=jnp.int32)
    ranked = random_bits * N_DP + jnp.arange(N_DP, dtype=jnp.int32)[None, :]
    order = jnp.argsort(ranked, axis=1)
    return order[:, :DOCS].astype(jnp.int32)


def raised(array, key, source, target, parts, factor):
    owner, partner = [(jnp.arange(array.shape[axis_at]) // (array.shape[axis_at] // parts)).reshape([-1 if axis == axis_at else 1 for axis in range(array.ndim)]) for axis_at in (source, target)]
    chosen = jax.random.permutation(key, parts)[partner]
    strong = (owner == chosen) | (owner == (partner + parts // 2) % parts)
    return jnp.where(strong, factor * array, array)


def shard_levels(own_key, dims, shards, least, high):
    level = 1.0
    for axis_at, shards_of in shards:
        steps = jax.random.uniform(jax.random.fold_in(jax.random.fold_in(own_key, 6), axis_at), (shards_of,), jnp.float32, least / len(shards), high / len(shards))
        level = level * jnp.repeat(jnp.exp(steps), dims[axis_at] // shards_of).reshape((-1,) + (1,) * (len(dims) - 1 - axis_at))
    return level


def split_up(number_of, total, most, lean):
    loads = [(1 << 20) // math.isqrt(rank ** lean) + 1 for rank in range(2, number_of + 1)]
    surplus, holding = total - most - (number_of - 1), [1] * (number_of - 1)
    while surplus > 0:
        candidates = [i for i in range(number_of - 1) if holding[i] < most]
        pool, remaining = sum([loads[i] for i in candidates]), surplus
        for i in candidates:
            addition = min(most - holding[i], max(1, remaining * loads[i] // pool), surplus)
            holding[i] = holding[i] + addition
            surplus = surplus - addition
    return np.array([most] + holding)


def ragged(rng, count, total, limit, skew):
    if count == 2:
        one = jax.random.randint(rng, (), max(1, total - limit), min(limit, total - 1) + 1)
        return jnp.stack([one, total - one])
    sizes = jnp.asarray(split_up(count, total, limit, skew), jnp.int32)
    couples = (count - 1) // 2
    source_of, taker = sizes[1:1 + 2 * couples:2], sizes[2:2 + 2 * couples:2]
    room = jnp.minimum(source_of - 1, limit - taker)
    moved = jax.random.randint(jax.random.fold_in(rng, 1), (couples,), 0, 1 << 20) % (room + 1)
    sizes = sizes.at[1:1 + 2 * couples:2].set(source_of - moved).at[2:2 + 2 * couples:2].set(taker + moved)
    return sizes[jax.random.permutation(jax.random.fold_in(rng, 2), count)]


def gaussian(key, extent, deviation, limit, split=(), kind=jnp.bfloat16):
    loudness = shard_levels(key, extent, split, -0.22, 0.18) if split else 1.0
    drawn = jax.random.normal(key, extent, jnp.float32) * deviation * loudness
    return jnp.minimum(jnp.maximum(drawn, -limit), limit).astype(kind)


def bell_draw_with(rng, extent, width, bound, pieces, heavy, kind=jnp.bfloat16):
    drawn = width * jax.random.normal(rng, extent, jnp.float32)
    if pieces:
        drawn = drawn * shard_levels(rng, extent, pieces, -0.22, 0.18)
    return jnp.clip(raised(drawn, jax.random.fold_in(rng, 3), *heavy), -bound, bound).astype(kind)


def setup_inputs(seed: int = 0) -> dict:
    seeds = jax.random.split(jax.random.key(seed), 8)
    queries = draw_queries(jax.random.fold_in(seeds[7], 71), 0)
    inputs = bell_draw_with(seeds[1], (TOKENS, D_WIN), 1.0, 24.0, ((0, 256),), (0, 1, 256, 6.0))
    key_weight = gaussian(seeds[2], (D_WIN, KV_WIDTH), D_WIN ** -0.5, 0.125, ((0, 8),))
    value_weight = gaussian(seeds[3], (D_WIN, KV_WIDTH), D_WIN ** -0.5, 0.125, ((0, 8),))
    lengths = jax.vmap(lambda own: ragged(own, DOCS, ROWS, SLOT, 2))(jax.random.split(seeds[4], (N_DP * N_FSDP))).reshape((N_DP * N_FSDP, DOCS)).astype(jnp.int32)
    doc_ranks = draw_doc_ranks(jax.random.fold_in(seeds[7], 71), 0)
    cotangent = gaussian(seeds[6], (N_DP * N_FSDP * BUFFER, Q_WIDTH), 1.0, 6.0, ((0, 256),))
    return dict(queries=queries, inputs=inputs, key_weight=key_weight, value_weight=value_weight, lengths=lengths, doc_ranks=doc_ranks, cotangent=cotangent)


def layout(doc_lengths, doc_route, row_count):
    doc_ends = jnp.cumsum(doc_lengths, dtype=jnp.int32)
    starts = doc_ends - doc_lengths
    tokens = jnp.arange(row_count, dtype=jnp.int32)
    inside = ((tokens[:, None] >= starts[None, :]) & (tokens[:, None] < doc_ends[None, :])).astype(jnp.int32)
    numbers = jnp.arange(doc_lengths.shape[0], dtype=jnp.int32)
    doc_index = jnp.sum(inside * numbers[None, :], axis=1, dtype=jnp.int32)
    position = tokens - jnp.sum(inside * starts[None, :], axis=1, dtype=jnp.int32)
    target = jnp.sum(inside * doc_route[None, :], axis=1, dtype=jnp.int32)
    return doc_index, position, target, starts


def rotary_tables(position, head_size):
    half_size = head_size // 2
    frequency = jnp.power(jnp.float32(500000.0), -2.0 * jnp.arange(half_size, dtype=jnp.float32) / head_size)
    angles = position.astype(jnp.float32)[:, None] * frequency[None, :]
    return jnp.cos(angles), jnp.sin(angles)


def rotate(matrix, cosine_table, sine_table, head_size, direction):
    row_count = matrix.shape[0]
    per_head = matrix.reshape(row_count, matrix.shape[1] // head_size, head_size)
    half_size = head_size // 2
    former = per_head[:, :, :half_size]
    latter = per_head[:, :, half_size:]
    cos_part = cosine_table[:, None, :]
    sin_part = sine_table[:, None, :]
    joined = jnp.concatenate([former * cos_part - direction * latter * sin_part, latter * cos_part + direction * former * sin_part], axis=2)
    return joined.reshape(row_count, matrix.shape[1])


def tile_grads(query_rows, key_rows, value_rows, grad_rows, query_doc, query_pos, key_doc, key_pos):
    row_count = query_rows.shape[0]
    key_count = key_rows.shape[0]
    kv_heads = key_rows.shape[1] // HEAD_DIM
    group_size = query_rows.shape[1] // key_rows.shape[1]
    factor = HEAD_DIM ** -0.5
    query_heads = query_rows.astype(jnp.float32).reshape(row_count, kv_heads, group_size, HEAD_DIM)
    grad_heads = grad_rows.astype(jnp.float32).reshape(row_count, kv_heads, group_size, HEAD_DIM)
    key_heads = key_rows.astype(jnp.float32).reshape(key_count, kv_heads, HEAD_DIM)
    value_heads = value_rows.astype(jnp.float32).reshape(key_count, kv_heads, HEAD_DIM)
    scores = jnp.einsum("tkgd,skd->kgts", query_heads, key_heads) * factor
    allowed = (key_doc[None, :] == query_doc[:, None]) & (key_pos[None, :] <= query_pos[:, None]) & (key_doc[None, :] >= 0)
    scores = jnp.where(allowed, scores, -1e30)
    row_max = jnp.max(scores, axis=-1, keepdims=True)
    expo_terms = jnp.where(allowed, jnp.exp(scores - row_max), 0.0)
    attn_probs = expo_terms / jnp.sum(expo_terms, axis=-1, keepdims=True)
    prob_half = attn_probs.astype(jnp.bfloat16).astype(jnp.float32)
    d_probs = jnp.einsum("tkgd,skd->kgts", grad_heads, value_heads)
    d_centre = jnp.sum(attn_probs * d_probs, axis=-1, keepdims=True)
    d_scores = (attn_probs * (d_probs - d_centre)).astype(jnp.bfloat16).astype(jnp.float32)
    d_query = jnp.einsum("kgts,skd->tkgd", d_scores, key_heads) * factor
    d_key = jnp.einsum("kgts,tkgd->skd", d_scores, query_heads) * factor
    d_value = jnp.einsum("kgts,tkgd->skd", prob_half, grad_heads)
    return d_query.reshape(row_count, -1), d_key.reshape(key_count, -1), d_value.reshape(key_count, -1)


def reference(queries, inputs, key_weight, value_weight, lengths, doc_ranks, cotangent):
    batches = N_DP * N_FSDP
    kv_weight = jnp.concatenate([key_weight, value_weight], axis=1)
    query_blocks = queries.reshape(batches, ROWS, Q_WIDTH)
    input_blocks = inputs.reshape(batches, ROWS, D_WIN)

    def one_batch(totals, number):
        key_total, value_total = totals
        query_rows = query_blocks[number]
        input_rows = input_blocks[number]
        doc_index, position, target, starts = layout(lengths[number], doc_ranks[number], ROWS)
        projected = jnp.dot(input_rows, kv_weight, preferred_element_type=jnp.float32)
        cosine_table, sine_table = rotary_tables(position, HEAD_DIM)
        key_vectors = rotate(projected[:, :KV_WIDTH], cosine_table, sine_table, HEAD_DIM, 1.0).astype(jnp.bfloat16)
        value_vectors = projected[:, KV_WIDTH:].astype(jnp.bfloat16)
        data_rank = number // N_FSDP
        shard_rank = number % N_FSDP
        source_rows = (target * N_FSDP + shard_rank) * BUFFER + data_rank * SLOT + position
        grad_rows = jnp.take(cotangent, source_rows.astype(jnp.int32), axis=0)
        d_query, d_key, d_value = tile_grads(query_rows, key_vectors, value_vectors, grad_rows, doc_index, position, doc_index, position)
        d_keys = d_key.astype(jnp.bfloat16)
        d_key_pre = rotate(d_keys.astype(jnp.float32), cosine_table, sine_table, HEAD_DIM, -1.0).astype(jnp.bfloat16)
        grad_kv = jnp.concatenate([d_key_pre, d_value.astype(jnp.bfloat16)], axis=1)
        d_input = jnp.dot(grad_kv, kv_weight.T, preferred_element_type=jnp.float32).astype(jnp.bfloat16)
        grad_partial = jnp.dot(input_rows.T, grad_kv, preferred_element_type=jnp.float32).astype(jnp.bfloat16)
        grad_partial = lax.optimization_barrier(grad_partial).astype(jnp.float32)
        key_total = key_total + grad_partial[:, :KV_WIDTH]
        value_total = value_total + grad_partial[:, KV_WIDTH:]
        return (key_total, value_total), (d_query.astype(jnp.bfloat16), d_input)

    initial = (jnp.zeros((D_WIN, KV_WIDTH), jnp.float32), jnp.zeros((D_WIN, KV_WIDTH), jnp.float32))
    (key_total, value_total), (query_grads, input_grads) = lax.scan(one_batch, initial, jnp.arange(batches, dtype=jnp.int32))
    factor = TOKENS ** -0.5
    return query_grads.reshape(TOKENS, Q_WIDTH), input_grads.reshape(TOKENS, D_WIN), key_total * factor, value_total * factor
```

```python
import jax
import jax.numpy as jnp
from jax import lax
from jax.sharding import PartitionSpec as P

HEAD_DIM = 128
SLOT = 24


def layout(doc_lengths, doc_route, row_count):
    doc_ends = jnp.cumsum(doc_lengths, dtype=jnp.int32)
    starts = doc_ends - doc_lengths
    tokens = jnp.arange(row_count, dtype=jnp.int32)
    inside = ((tokens[:, None] >= starts[None, :]) & (tokens[:, None] < doc_ends[None, :])).astype(
        jnp.int32
    )
    numbers = jnp.arange(doc_lengths.shape[0], dtype=jnp.int32)
    doc_index = jnp.sum(inside * numbers[None, :], axis=1, dtype=jnp.int32)
    position = tokens - jnp.sum(inside * starts[None, :], axis=1, dtype=jnp.int32)
    target = jnp.sum(inside * doc_route[None, :], axis=1, dtype=jnp.int32)
    return doc_index, position, target


def rotary_tables(position, head_size):
    half_size = head_size // 2
    frequency = jnp.power(
        jnp.float32(500000.0), -2.0 * jnp.arange(half_size, dtype=jnp.float32) / head_size
    )
    angles = position.astype(jnp.float32)[:, None] * frequency[None, :]
    return jnp.cos(angles), jnp.sin(angles)


def rotate(matrix, cosine_table, sine_table, head_size, direction):
    row_count = matrix.shape[0]
    per_head = matrix.reshape(row_count, matrix.shape[1] // head_size, head_size)
    half_size = head_size // 2
    former = per_head[:, :, :half_size]
    latter = per_head[:, :, half_size:]
    cos_part = cosine_table[:, None, :]
    sin_part = sine_table[:, None, :]
    joined = jnp.concatenate(
        [
            former * cos_part - direction * latter * sin_part,
            latter * cos_part + direction * former * sin_part,
        ],
        axis=2,
    )
    return joined.reshape(row_count, matrix.shape[1])


def head_grads(query_rows, key_rows, value_rows, grad_rows, allowed):
    count = query_rows.shape[0]
    group = query_rows.shape[1] // HEAD_DIM
    factor = HEAD_DIM ** (-0.5)
    stacked_q = jnp.concatenate(
        [query_rows[:, h * HEAD_DIM : (h + 1) * HEAD_DIM] for h in range(group)], axis=0
    )
    stacked_g = jnp.concatenate(
        [grad_rows[:, h * HEAD_DIM : (h + 1) * HEAD_DIM] for h in range(group)], axis=0
    )
    allowed = jnp.concatenate([allowed] * group, axis=0)
    across = (((1,), (1,)), ((), ()))
    down = (((0,), (0,)), ((), ()))
    scores = lax.dot_general(stacked_q, key_rows, across, preferred_element_type=jnp.float32)
    scores = jnp.where(allowed, scores * factor, -1e30)
    expo = jnp.exp(scores - jnp.max(scores, axis=-1, keepdims=True))
    probs = expo / jnp.sum(expo, axis=-1, keepdims=True)
    d_probs = lax.dot_general(stacked_g, value_rows, across, preferred_element_type=jnp.float32)
    centre = jnp.sum(probs * d_probs, axis=-1, keepdims=True)
    d_scores = (probs * (d_probs - centre)).astype(jnp.bfloat16)
    d_query = jnp.dot(d_scores, key_rows, preferred_element_type=jnp.float32) * factor
    d_key = lax.dot_general(d_scores, stacked_q, down, preferred_element_type=jnp.float32) * factor
    d_value = lax.dot_general(
        probs.astype(jnp.bfloat16), stacked_g, down, preferred_element_type=jnp.float32
    )
    d_query = jnp.concatenate(
        [d_query[h * count : (h + 1) * count] for h in range(group)], axis=1
    )
    return d_query, d_key, d_value


def body(queries, inputs, key_weight, value_weight, lengths, doc_ranks, cotangent):
    row_count = inputs.shape[0]
    data_size = lax.axis_size("dp")
    shard_size = lax.axis_size("fsdp")
    kv_cols = key_weight.shape[1]
    heads = kv_cols // HEAD_DIM
    arrived = lax.all_to_all(
        cotangent.reshape(data_size, SLOT, -1), "dp", split_axis=0, concat_axis=0
    ).reshape(data_size * SLOT, -1)
    doc_index, position, target = layout(lengths[0], doc_ranks[0], row_count)
    combined = jnp.concatenate([key_weight, value_weight], axis=1)
    full_weight = lax.all_gather(combined, "fsdp", axis=0, tiled=True)
    projected = jnp.dot(inputs, full_weight, preferred_element_type=jnp.float32)
    cosine_table, sine_table = rotary_tables(position, HEAD_DIM)
    key_vectors = rotate(projected[:, :kv_cols], cosine_table, sine_table, HEAD_DIM, 1.0).astype(
        jnp.bfloat16
    )
    value_vectors = projected[:, kv_cols:].astype(jnp.bfloat16)
    picked = (
        (target * SLOT + position)[:, None] == jnp.arange(data_size * SLOT, dtype=jnp.int32)[None]
    ).astype(jnp.bfloat16)
    grad_rows = jnp.dot(picked, arrived, preferred_element_type=jnp.float32).astype(jnp.bfloat16)
    allowed = (doc_index[:, None] == doc_index[None, :]) & (
        position[None, :] <= position[:, None]
    )
    width = queries.shape[1] // heads
    d_query, d_key, d_value = [], [], []
    for g in range(heads):
        one = head_grads(
            queries[:, g * width : (g + 1) * width],
            key_vectors[:, g * HEAD_DIM : (g + 1) * HEAD_DIM],
            value_vectors[:, g * HEAD_DIM : (g + 1) * HEAD_DIM],
            grad_rows[:, g * width : (g + 1) * width],
            allowed,
        )
        d_query.append(one[0])
        d_key.append(one[1])
        d_value.append(one[2])
    d_queries = jnp.concatenate(d_query, axis=1).astype(jnp.bfloat16)
    d_keys = jnp.concatenate(d_key, axis=1).astype(jnp.bfloat16)
    d_values = jnp.concatenate(d_value, axis=1).astype(jnp.bfloat16)
    d_key_pre = rotate(
        d_keys.astype(jnp.float32), cosine_table, sine_table, HEAD_DIM, -1.0
    ).astype(jnp.bfloat16)
    grad_kv = jnp.concatenate([d_key_pre, d_values], axis=1)
    block_rows = inputs.shape[1] // (data_size * shard_size)
    by_shard = (
        inputs.reshape(row_count, data_size, shard_size, block_rows)
        .transpose(0, 2, 1, 3)
        .reshape(row_count, -1)
    )
    grad_partial = lax.dot_general(
        by_shard, grad_kv, (((0,), (0,)), ((), ())), preferred_element_type=jnp.float32
    ).astype(jnp.bfloat16)
    shard_sums = lax.psum_scatter(grad_partial, "fsdp", scatter_dimension=0, tiled=True)
    final_sums = lax.psum_scatter(
        shard_sums.astype(jnp.float32), "dp", scatter_dimension=0, tiled=True
    )
    d_inputs = lax.dot_general(
        grad_kv, full_weight, (((1,), (1,)), ((), ())), preferred_element_type=jnp.float32
    ).astype(jnp.bfloat16)
    factor = (row_count * data_size * shard_size) ** (-0.5)
    return (
        d_queries,
        d_inputs,
        final_sums[:, :kv_cols] * factor,
        final_sums[:, kv_cols:] * factor,
    )


def solution(mesh):
    both = P(("dp", "fsdp"), None)
    placed = (both, both, P("fsdp", None), P("fsdp", None), both, both, both)
    return jax.shard_map(
        body, mesh=mesh, in_specs=placed, out_specs=(both,) * 4, check_vma=False
    )
```

```python
import functools
import math

import jax
import jax.numpy as jnp
from jax import lax
from jax.experimental import pallas as pl
from jax.experimental.pallas import tpu as pltpu
from jax.sharding import PartitionSpec as P

HEAD_DIM = 128
SLOT = 24
SUB = 8
CORES = 2
THETA = 500000.0
MESH = pl.DeviceIdType.MESH
ACROSS = (((1,), (1,)), ((), ()))
DOWN = (((0,), (0,)), ((), ()))


def dot(a, b, dims=(((1,), (0,)), ((), ()))):
    return lax.dot_general(a, b, dims, preferred_element_type=jnp.float32)


def kernel(
    sizes,
    q_any,
    in_any,
    kw_any,
    vw_any,
    len_ref,
    rank_ref,
    cot_any,
    dq_ref,
    di_ref,
    dkw_ref,
    dvw_ref,
    q_ref,
    in_ref,
    w_ref,
    cot_refs,
    proj_ref,
    key_ref,
    val_ref,
    prob_ref,
    turned_ref,
    pair_ref,
    grad_ref,
    s1_ref,
    r1_ref,
    s2_ref,
    r2_ref,
    s3_ref,
    r3_ref,
    load_sem,
    own_sem,
    cot_send,
    cot_recv,
    ring_send,
    ring_recv,
    twin_send,
    twin_recv,
    turn_sem,
    grad_send,
    grad_recv,
    send1,
    recv1,
    send2,
    recv2,
    send3,
    recv3,
):
    n_dp, y_size, x_size, z_size, heads = sizes
    me = lax.axis_index("dp")
    z = lax.axis_index("fsdp")
    core = lax.rem(me, CORES)
    x = lax.rem(me // CORES, x_size)
    y = me // (CORES * x_size)
    twin = me + 1 - 2 * core
    tokens = q_ref.shape[0]
    width = q_ref.shape[1] // heads
    group = width // HEAD_DIM
    kv_cols = heads * HEAD_DIM
    shard_rows = w_ref.shape[2]
    docs = len_ref.shape[1]
    half = z_size // 2
    factor = HEAD_DIM ** (-0.5)

    def at(dp, fsdp):
        return {"dp": dp, "fsdp": fsdp}

    def remote(src, dst, send, recv, device):
        return pltpu.make_async_remote_copy(
            src_ref=src,
            dst_ref=dst,
            send_sem=send,
            recv_sem=recv,
            device_id=device,
            device_id_type=MESH,
        )

    loads = [
        pltpu.make_async_copy(kw_any, w_ref.at[z, 0], load_sem.at[0]),
        pltpu.make_async_copy(vw_any, w_ref.at[z, 1], load_sem.at[1]),
        pltpu.make_async_copy(in_any, in_ref, load_sem.at[2]),
        pltpu.make_async_copy(q_any, q_ref, load_sem.at[3]),
    ]
    for load in loads:
        load.start()
    own_cot = [
        pltpu.make_async_copy(
            cot_any.at[me, :, :, pl.ds(g * width, width)], cot_refs[g].at[me], own_sem.at[g]
        )
        for g in range(heads)
    ]

    barrier = pltpu.get_barrier_semaphore()

    def greet_dp(s, carry):
        to = lax.rem(me + s, n_dp)
        pl.semaphore_signal(barrier, inc=1, device_id=at(to, z), device_id_type=MESH)
        return carry

    def greet_fsdp(s, carry):
        to = lax.rem(z + s, z_size)
        pl.semaphore_signal(barrier, inc=1, device_id=at(me, to), device_id_type=MESH)
        return carry

    lax.fori_loop(1, n_dp, greet_dp, 0)
    lax.fori_loop(1, z_size, greet_fsdp, 0)
    pl.semaphore_wait(barrier, n_dp - 1 + z_size - 1)

    def part(way, step):
        shard = lax.rem(z + (z_size - step if way == 0 else step), z_size)
        if step < half:
            return shard, pl.ds(0, shard_rows)
        return shard, pl.ds(way * (shard_rows // 2), shard_rows // 2)

    def ring_hop(way, step):
        shard = lax.rem(z + (z_size - step + 1 if way == 0 else step - 1), z_size)
        rows = part(way, step)[1]
        to = lax.rem(z + (1 if way == 0 else z_size - 1), z_size)
        place = w_ref.at[shard, core, rows]
        return remote(
            place, place, ring_send.at[way, step - 1], ring_recv.at[way, step - 1], at(me, to)
        )

    def ring_arrival(way, step):
        shard, rows = part(way, step)
        place = w_ref.at[shard, core, rows]
        return remote(
            place, place, ring_send.at[way, step - 1], ring_recv.at[way, step - 1], at(me, z)
        )

    def twin_copy(way, step, kind):
        shard, rows = part(way, step)
        place = w_ref.at[shard, kind, rows]
        return remote(
            place, place, twin_send.at[way, step - 1], twin_recv.at[way, step - 1], at(twin, z)
        )

    loads[0].wait()
    loads[1].wait()
    for way in range(2):
        ring_hop(way, 1).start()

    def send_cot(g):
        def one(s, carry):
            to = lax.rem(me + s, n_dp)
            remote(
                cot_any.at[to, :, :, pl.ds(g * width, width)],
                cot_refs[g].at[me],
                cot_send.at[g],
                cot_recv.at[g],
                at(to, z),
            ).start()
            return carry

        lax.fori_loop(1, n_dp, one, 0)
        own_cot[g].start()

    for g in range(heads):
        send_cot(g)

    loads[2].wait()
    loads[3].wait()

    blocks = y_size * x_size
    block = in_ref.shape[1] // (blocks * CORES)
    for b in range(blocks):
        turned = in_ref[:, b * CORES * block : (b + 1) * CORES * block].astype(jnp.float32).T
        turned = turned.astype(jnp.bfloat16)
        for c in range(CORES):
            turned_ref[c, b * block : (b + 1) * block, :] = turned[c * block : (c + 1) * block]
    turn_own = pltpu.make_async_copy(
        turned_ref.at[core], pair_ref.at[:, pl.ds(0, tokens)], turn_sem.at[0]
    )
    turn_twin = remote(
        turned_ref.at[1 - core],
        pair_ref.at[:, pl.ds(tokens, tokens)],
        turn_sem.at[1],
        turn_sem.at[2],
        at(twin, z),
    )
    turn_own.start()
    turn_twin.start()

    def project(shard, first):
        cols = pl.ds(pl.multiple_of(shard * shard_rows, shard_rows), shard_rows)
        rows = in_ref[:, cols]
        for kind in range(2):
            out = slice(kind * kv_cols, (kind + 1) * kv_cols)
            term = dot(rows, w_ref[shard, kind])
            if first:
                proj_ref[:, out] = term
            else:
                proj_ref[:, out] += term

    project(z, True)
    for step in range(1, half + 1):
        for way in range(2):
            ring_arrival(way, step).wait_recv()
            if step < half:
                ring_hop(way, step + 1).start()
            twin_copy(way, step, core).start()
        for way in range(2):
            twin_copy(way, step, 1 - core).wait_recv()
            if step < half:
                project(part(way, step)[0], False)
        if step == half:
            project(part(0, step)[0], False)

    def spread(shape, axis):
        token = lax.broadcasted_iota(jnp.int32, shape, axis)
        doc = jnp.zeros(shape, jnp.int32)
        start = jnp.zeros(shape, jnp.int32)
        end = jnp.int32(0)
        for k in range(docs - 1):
            length = len_ref[0, k]
            end = end + length
            past = token >= end
            doc = doc + jnp.where(past, 1, 0)
            start = start + jnp.where(past, length, 0)
        return token, doc, token - start

    square = (tokens, tokens)
    token0, doc0, pos0 = spread(square, 0)
    token1, doc1, _ = spread(square, 1)
    allowed = (doc0 == doc1) & (token1 <= token0)
    allowed = jnp.concatenate([allowed.astype(jnp.float32)] * group, axis=0) > 0.5
    table = (tokens, HEAD_DIM)
    _, _, place = spread(table, 0)
    lane = lax.broadcasted_iota(jnp.int32, table, 1)
    pair = jnp.where(lane < HEAD_DIM // 2, lane, lane - HEAD_DIM // 2).astype(jnp.float32)
    frequency = jnp.exp(pair * jnp.float32(-2.0 * math.log(THETA) / HEAD_DIM))
    angle = place.astype(jnp.float32) * frequency
    cosine = jnp.cos(angle)
    sine = jnp.sin(angle)
    sine = jnp.where(lane < HEAD_DIM // 2, -sine, sine)
    _, doc_s, pos_s = spread((tokens, docs * SLOT), 0)
    column = lax.broadcasted_iota(jnp.int32, (tokens, docs * SLOT), 1)
    picked = jnp.where(doc_s * SLOT + pos_s == column, 1.0, 0.0).astype(jnp.bfloat16)

    def turn(rows, direction):
        return rows * cosine + direction * pltpu.roll(rows, HEAD_DIM // 2, 1) * sine

    def stack(rows):
        return jnp.concatenate(
            [rows[:, h * HEAD_DIM : (h + 1) * HEAD_DIM] for h in range(group)], axis=0
        )

    for g in range(heads):
        cols = slice(g * HEAD_DIM, (g + 1) * HEAD_DIM)
        keys = turn(proj_ref[:, cols], 1.0).astype(jnp.bfloat16)
        key_ref[g] = keys
        val_ref[g] = proj_ref[:, kv_cols + g * HEAD_DIM : kv_cols + (g + 1) * HEAD_DIM].astype(
            jnp.bfloat16
        )
        queries = stack(q_ref[:, g * width : (g + 1) * width])
        scores = jnp.where(allowed, dot(queries, keys, ACROSS) * factor, -1e30)
        expo = jnp.exp(scores - jnp.max(scores, axis=-1, keepdims=True))
        prob_ref[g] = expo / jnp.sum(expo, axis=-1, keepdims=True)

    def peer1(kind, index):
        return at(me + (index - x) * CORES, z) if kind == 0 else at(
            me + (index - y) * CORES * x_size, z
        )

    def peer2(kind, index):
        return peer1(1 - kind, index)

    count1 = (x_size, y_size)
    count2 = (y_size, x_size)
    mine1 = (x, y)
    mine2 = (y, x)

    def start1(g):
        for kind in range(2):
            for s in range(1, count1[kind]):
                to = lax.rem(mine1[kind] + s, count1[kind])
                remote(
                    s1_ref[kind].at[g, to],
                    r1_ref[kind].at[g, mine1[kind]],
                    send1.at[g, kind],
                    recv1.at[g, kind],
                    peer1(kind, to),
                ).start()

    def all1(g, kind):
        some = r1_ref[kind].at[g, pl.ds(0, count1[kind] - 1)]
        return remote(some, some, send1.at[g, kind], recv1.at[g, kind], at(twin, z))

    def start2(g):
        for kind in range(2):
            all1(g, kind).wait_recv()
            own = mine1[kind]
            total = s1_ref[kind][g, own].astype(jnp.float32)
            for s in range(1, count1[kind]):
                total += r1_ref[kind][g, lax.rem(own + s, count1[kind])].astype(jnp.float32)
            s2_ref[kind][g] = total.astype(jnp.bfloat16)
            for s in range(1, count2[kind]):
                to = lax.rem(mine2[kind] + s, count2[kind])
                remote(
                    s2_ref[kind].at[g, to],
                    r2_ref[kind].at[g, mine2[kind]],
                    send2.at[g, kind],
                    recv2.at[g, kind],
                    peer2(kind, to),
                ).start()

    def all2(g, kind):
        some = r2_ref[kind].at[g, pl.ds(0, count2[kind] - 1)]
        return remote(some, some, send2.at[g, kind], recv2.at[g, kind], at(twin, z))

    def start3(g):
        for kind in range(2):
            all2(g, kind).wait_recv()
            own = mine2[kind]
            total = s2_ref[kind][g, own].astype(jnp.float32)
            for s in range(1, count2[kind]):
                total += r2_ref[kind][g, lax.rem(own + s, count2[kind])].astype(jnp.float32)
            s3_ref[g, :, :, kind * HEAD_DIM : (kind + 1) * HEAD_DIM] = total.reshape(
                z_size, block // z_size, HEAD_DIM
            )
        for s in range(1, z_size):
            to = lax.rem(z + s, z_size)
            remote(
                s3_ref.at[g, to], r3_ref.at[g, z], send3.at[g], recv3.at[g], at(me, to)
            ).start()

    def all3(g):
        some = r3_ref.at[g, pl.ds(0, z_size - 1)]
        return remote(some, some, send3.at[g], recv3.at[g], at(twin, z))

    def finish(g):
        all3(g).wait_recv()
        total = s3_ref[g, z]
        for s in range(1, z_size):
            total += r3_ref[g, lax.rem(z + s, z_size)]
        total = total * jnp.float32((tokens * n_dp * z_size) ** (-0.5))
        dkw_ref[:, g * HEAD_DIM : (g + 1) * HEAD_DIM] = total[:, :HEAD_DIM]
        dvw_ref[:, g * HEAD_DIM : (g + 1) * HEAD_DIM] = total[:, HEAD_DIM:]

    def all_cot(g):
        some = cot_refs[g].at[pl.ds(0, n_dp - 1)]
        return remote(some, some, cot_send.at[g], cot_recv.at[g], at(twin, z))

    def grad_copy(g):
        return remote(
            grad_ref.at[g, pl.ds(0, tokens)],
            grad_ref.at[g, pl.ds(tokens, tokens)],
            grad_send.at[g],
            grad_recv.at[g],
            at(twin, z),
        )

    for g in range(heads):
        own_cot[g].wait()
        all_cot(g).wait_recv()
        slots = jnp.concatenate(
            [
                cot_refs[g][rank_ref[0, k]].astype(jnp.float32).reshape(SLOT, width)
                for k in range(docs)
            ],
            axis=0,
        ).astype(jnp.bfloat16)
        grads = stack(dot(picked, slots).astype(jnp.bfloat16))
        queries = stack(q_ref[:, g * width : (g + 1) * width])
        probs = prob_ref[g]
        d_probs = dot(grads, val_ref[g], ACROSS)
        centre = jnp.sum(probs * d_probs, axis=-1, keepdims=True)
        d_scores = (probs * (d_probs - centre)).astype(jnp.bfloat16)
        d_keys = (dot(d_scores, queries, DOWN) * factor).astype(jnp.bfloat16)
        d_values = dot(probs.astype(jnp.bfloat16), grads, DOWN).astype(jnp.bfloat16)
        d_key_pre = turn(d_keys.astype(jnp.float32), -1.0).astype(jnp.bfloat16)
        grad_ref[g, :tokens, :HEAD_DIM] = d_key_pre
        grad_ref[g, :tokens, HEAD_DIM:] = d_values
        grad_copy(g).start()
        d_queries = (dot(d_scores, key_ref[g]) * factor).astype(jnp.bfloat16)
        for h in range(group):
            dq_ref[:, g * width + h * HEAD_DIM : g * width + (h + 1) * HEAD_DIM] = d_queries[
                h * tokens : (h + 1) * tokens
            ]
        if g >= 1:
            start2(g - 1)
        if g >= 2:
            start3(g - 2)
        if g == 0:
            turn_own.wait()
            turn_twin.wait_recv()
        grad_copy(g).wait_recv()
        partial = dot(pair_ref[...], grad_ref[g]).astype(jnp.bfloat16)
        for b in range(blocks):
            by, bx = b // x_size, b % x_size
            rows = partial[b * block : (b + 1) * block]
            s1_ref[0][g, bx, by] = rows[:, :HEAD_DIM]
            s1_ref[1][g, by, bx] = rows[:, HEAD_DIM:]
        start1(g)

    keys_side = jnp.concatenate([grad_ref[g, :tokens, :HEAD_DIM] for g in range(heads)], axis=1)
    values_side = jnp.concatenate([grad_ref[g, :tokens, HEAD_DIM:] for g in range(heads)], axis=1)
    for j in range(z_size):
        rows = dot(keys_side, w_ref[j, 0], ACROSS) + dot(values_side, w_ref[j, 1], ACROSS)
        di_ref[:, j * shard_rows : (j + 1) * shard_rows] = rows.astype(jnp.bfloat16)

    last = heads - 1
    start2(last)
    if heads >= 2:
        start3(last - 1)
    start3(last)
    for g in range(heads):
        finish(g)

    for step in range(1, half + 1):
        for way in range(2):
            ring_hop(way, step).wait_send()
            twin_copy(way, step, core).wait_send()
    turn_twin.wait_send()
    for g in range(heads):
        all_cot(g).wait_send()
        grad_copy(g).wait_send()
        all3(g).wait_send()
        for kind in range(2):
            all1(g, kind).wait_send()
            all2(g, kind).wait_send()


def body(queries, inputs, key_weight, value_weight, lengths, doc_ranks, cotangent):
    n_dp = lax.axis_size("dp")
    z_size = lax.axis_size("fsdp")
    x_size = 4 if n_dp >= 32 else 2
    y_size = n_dp // (CORES * x_size)
    tokens, channels = inputs.shape
    shard_rows, kv_cols = key_weight.shape
    heads = kv_cols // HEAD_DIM
    width = queries.shape[1] // heads
    block = channels // (n_dp)
    own_rows = channels // (n_dp * z_size)
    steps = z_size // 2
    bf16, f32 = jnp.bfloat16, jnp.float32
    any_spec = pl.BlockSpec(memory_space=pl.ANY)
    smem = pl.BlockSpec(memory_space=pltpu.SMEM)
    vmem = pl.BlockSpec(memory_space=pltpu.VMEM)
    dma = pltpu.SemaphoreType.DMA

    def entry(*refs):
        refs = list(refs)
        head, cots, rest = refs[:14], refs[14 : 14 + heads], refs[14 + heads :]
        pairs = [rest[7 + 2 * i : 9 + 2 * i] for i in range(4)]
        sizes = (n_dp, y_size, x_size, z_size, heads)
        kernel(sizes, *head, cots, *rest[:7], *pairs, *rest[15:])

    scratch = [
        pltpu.VMEM((tokens, queries.shape[1]), bf16),
        pltpu.VMEM((tokens, channels), bf16),
        pltpu.VMEM((z_size, 2, shard_rows, kv_cols), bf16),
        *[pltpu.VMEM((n_dp, SLOT // SUB, SUB, width), bf16) for _ in range(heads)],
        pltpu.VMEM((tokens, 2 * kv_cols), f32),
        pltpu.VMEM((heads, tokens, HEAD_DIM), bf16),
        pltpu.VMEM((heads, tokens, HEAD_DIM), bf16),
        pltpu.VMEM((heads, tokens * width // HEAD_DIM, tokens), f32),
        pltpu.VMEM((CORES, channels // CORES, tokens), bf16),
        pltpu.VMEM((channels // CORES, CORES * tokens), bf16),
        pltpu.VMEM((heads, CORES * tokens, 2 * HEAD_DIM), bf16),
        pltpu.VMEM((heads, x_size, y_size, block, HEAD_DIM), bf16),
        pltpu.VMEM((heads, y_size, x_size, block, HEAD_DIM), bf16),
        pltpu.VMEM((heads, x_size, y_size, block, HEAD_DIM), bf16),
        pltpu.VMEM((heads, y_size, x_size, block, HEAD_DIM), bf16),
        pltpu.VMEM((heads, y_size, block, HEAD_DIM), bf16),
        pltpu.VMEM((heads, x_size, block, HEAD_DIM), bf16),
        pltpu.VMEM((heads, y_size, block, HEAD_DIM), bf16),
        pltpu.VMEM((heads, x_size, block, HEAD_DIM), bf16),
        pltpu.VMEM((heads, z_size, own_rows, 2 * HEAD_DIM), f32),
        pltpu.VMEM((heads, z_size, own_rows, 2 * HEAD_DIM), f32),
        dma((4,)),
        dma((heads,)),
        dma((heads,)),
        dma((heads,)),
        dma((2, steps)),
        dma((2, steps)),
        dma((2, steps)),
        dma((2, steps)),
        dma((3,)),
        dma((heads,)),
        dma((heads,)),
        dma((heads, 2)),
        dma((heads, 2)),
        dma((heads, 2)),
        dma((heads, 2)),
        dma((heads,)),
        dma((heads,)),
    ]
    flops = 2 * tokens * channels * 2 * kv_cols * 4
    return pl.pallas_call(
        entry,
        out_shape=(
            jax.ShapeDtypeStruct(queries.shape, bf16),
            jax.ShapeDtypeStruct(inputs.shape, bf16),
            jax.ShapeDtypeStruct((own_rows, kv_cols), f32),
            jax.ShapeDtypeStruct((own_rows, kv_cols), f32),
        ),
        in_specs=[any_spec] * 4 + [smem] * 2 + [any_spec],
        out_specs=(vmem,) * 4,
        scratch_shapes=scratch,
        cost_estimate=pl.CostEstimate(
            flops=flops, bytes_accessed=8 * cotangent.size, transcendentals=0
        ),
        compiler_params=pltpu.CompilerParams(
            collective_id=0, has_side_effects=True, vmem_limit_bytes=48 * 1024 * 1024
        ),
    )(
        queries,
        inputs,
        key_weight,
        value_weight,
        lengths,
        doc_ranks,
        cotangent.reshape(n_dp, SLOT // SUB, SUB, cotangent.shape[1]),
    )


def solution(mesh):
    both = P(("dp", "fsdp"), None)
    placed = (both, both, P("fsdp", None), P("fsdp", None), both, both, both)
    return jax.shard_map(
        body, mesh=mesh, in_specs=placed, out_specs=(both,) * 4, check_vma=False
    )
```

```python
import functools
import math

import jax
import jax.numpy as jnp
from jax import lax
from jax.experimental import pallas as pl
from jax.experimental.pallas import tpu as pltpu
from jax.sharding import PartitionSpec as P

HEAD_DIM = 128
SLOT = 24
SUB = 8
PIECES = 4
CORES = 2
THETA = 500000.0
MESH = pl.DeviceIdType.MESH
ACROSS = (((1,), (1,)), ((), ()))
DOWN = (((0,), (0,)), ((), ()))


def dot(a, b, dims=(((1,), (0,)), ((), ()))):
    return lax.dot_general(a, b, dims, preferred_element_type=jnp.float32)


def kernel(
    sizes,
    q_any,
    in_any,
    kw_any,
    vw_any,
    len_ref,
    rank_ref,
    cot_any,
    dq_any,
    di_any,
    dkw_any,
    dvw_any,
    q_ref,
    in_ref,
    w_ref,
    cot_refs,
    proj_ref,
    key_ref,
    val_ref,
    prob_ref,
    turned_ref,
    pair_ref,
    grad_ref,
    dq_ref,
    di_ref,
    dkw_ref,
    dvw_ref,
    s1_ref,
    r1_ref,
    s2_ref,
    r2_ref,
    s3_ref,
    r3_ref,
    load_sem,
    own_sem,
    cot_send,
    cot_recv,
    ring_send,
    ring_recv,
    twin_send,
    twin_recv,
    turn_sem,
    grad_send,
    grad_recv,
    send1,
    recv1,
    send2,
    recv2,
    send3,
    recv3,
    gate,
    out_sem,
):
    n_dp, y_size, x_size, z_size, heads = sizes
    me = lax.axis_index("dp")
    z = lax.axis_index("fsdp")
    core = lax.rem(me, CORES)
    x = lax.rem(me // CORES, x_size)
    y = me // (CORES * x_size)
    twin = me + 1 - 2 * core
    tokens = q_ref.shape[0]
    width = q_ref.shape[1] // heads
    group = width // HEAD_DIM
    kv_cols = heads * HEAD_DIM
    shard_rows = w_ref.shape[2]
    docs = len_ref.shape[1]
    half = z_size // 2
    factor = HEAD_DIM ** (-0.5)

    right = lax.rem(z + 1, z_size)
    left = lax.rem(z + z_size - 1, z_size)

    def at(dp, fsdp):
        return {"dp": dp, "fsdp": fsdp}

    def at_x(s):
        return me + (lax.rem(x + s, x_size) - x) * CORES

    def at_y(s):
        return me + (lax.rem(y + s, y_size) - y) * CORES * x_size

    def remote(src, dst, send, recv, device):
        return pltpu.make_async_remote_copy(
            src_ref=src,
            dst_ref=dst,
            send_sem=send,
            recv_sem=recv,
            device_id=device,
            device_id_type=MESH,
        )

    loads = [
        pltpu.make_async_copy(kw_any, w_ref.at[z, 0], load_sem.at[0]),
        pltpu.make_async_copy(vw_any, w_ref.at[z, 1], load_sem.at[1]),
        pltpu.make_async_copy(in_any, in_ref, load_sem.at[2]),
        pltpu.make_async_copy(q_any, q_ref, load_sem.at[3]),
    ]
    for load in loads:
        load.start()
    own_cot = [
        pltpu.make_async_copy(
            cot_any.at[me, :, :, pl.ds(g * width, width)], cot_refs[g].at[me], own_sem.at[g]
        )
        for g in range(heads)
    ]

    barrier = pltpu.get_barrier_semaphore()
    around = [(at_x(s), z) for s in range(1, x_size)] + [(at_y(s), z) for s in range(1, y_size)]
    around += [(twin, z)] + [(me, to) for to in (right, left)][: z_size - 1]
    for dp, fsdp in around:
        pl.semaphore_signal(barrier, inc=1, device_id=at(dp, fsdp), device_id_type=MESH)
    pl.semaphore_wait(barrier, len(around))

    def pieces(way, step):
        if step < half:
            return list(range(PIECES))
        return list(range(way * PIECES // 2, (way + 1) * PIECES // 2))

    def shard_at(way, step):
        return lax.rem(z + (z_size - step if way == 0 else step), z_size)

    def place_at(way, step, k, kind):
        rows = pl.ds(k * (shard_rows // PIECES), shard_rows // PIECES)
        return w_ref.at[shard_at(way, step), kind, rows]

    def ring_copy(place, way, step, k, device):
        sems = (ring_send.at[way, step - 1, k], ring_recv.at[way, step - 1, k])
        return remote(place, place, *sems, device)

    def ring_hop(way, step, k):
        return ring_copy(
            place_at(way, step - 1, k, core), way, step, k, at(me, right if way == 0 else left)
        )

    def ring_arrival(way, step, k):
        return ring_copy(place_at(way, step, k, core), way, step, k, at(twin, z))

    def twin_copy(way, step, k, kind):
        place = place_at(way, step, k, kind)
        sems = (twin_send.at[way, step - 1, k], twin_recv.at[way, step - 1, k])
        return remote(place, place, *sems, at(twin, z))

    def relay(step):
        for k in range(PIECES):
            for way in range(2):
                if k not in pieces(way, step):
                    continue
                ring_arrival(way, step, k).wait_recv()
                if step < half and k in pieces(way, step + 1):
                    ring_hop(way, step + 1, k).start()
                twin_copy(way, step, k, core).start()

    def from_twin(step):
        for way in range(2):
            for k in pieces(way, step):
                twin_copy(way, step, k, 1 - core).wait_recv()

    loads[0].wait()
    loads[1].wait()
    for k in range(PIECES):
        for way in range(2):
            if k in pieces(way, 1):
                ring_hop(way, 1, k).start()

    for s in range(1, y_size):
        pl.semaphore_signal(gate.at[0], inc=1, device_id=at(at_y(s), z), device_id_type=MESH)
    pl.semaphore_wait(gate.at[0], y_size - 1)
    pl.semaphore_signal(gate.at[1], inc=1, device_id=at(twin, z), device_id_type=MESH)

    def send_cot(g, first, last, base, stride):
        def one(s, carry):
            to = lax.rem(base + stride * s, n_dp)
            remote(
                cot_any.at[to, :, :, pl.ds(g * width, width)],
                cot_refs[g].at[me],
                cot_send.at[g],
                cot_recv.at[g],
                at(to, z),
            ).start()
            return carry

        lax.fori_loop(first, last, one, 0)

    send_cot(0, 1, n_dp // CORES, me, CORES)
    pl.semaphore_wait(gate.at[1], 1)
    send_cot(0, 0, n_dp // CORES, twin, CORES)
    for g in range(heads):
        own_cot[g].start()

    loads[2].wait()
    loads[3].wait()

    def project(shard, first=False):
        cols = pl.ds(pl.multiple_of(shard * shard_rows, shard_rows), shard_rows)
        rows = in_ref[:, cols]
        for kind in range(2):
            out = slice(kind * kv_cols, (kind + 1) * kv_cols)
            term = dot(rows, w_ref[shard, kind])
            if first:
                proj_ref[:, out] = term
            else:
                proj_ref[:, out] += term

    def project_step(step):
        if step == 0:
            project(z, True)
            return
        from_twin(step)
        for way in range(2 if step < half else 1):
            project(shard_at(way, step))

    blocks = y_size * x_size
    block = in_ref.shape[1] // (blocks * CORES)

    def turn_block(b):
        turned = in_ref[:, b * CORES * block : (b + 1) * CORES * block].astype(jnp.float32).T
        turned = turned.astype(jnp.bfloat16)
        for c in range(CORES):
            turned_ref[c, b * block : (b + 1) * block, :] = turned[c * block : (c + 1) * block]

    turn_own = pltpu.make_async_copy(
        turned_ref.at[core], pair_ref.at[:, pl.ds(0, tokens)], turn_sem.at[0]
    )
    turn_twin = remote(
        turned_ref.at[1 - core],
        pair_ref.at[:, pl.ds(tokens, tokens)],
        turn_sem.at[1],
        turn_sem.at[2],
        at(twin, z),
    )

    chunk, turned_blocks = 1, 0
    for step in range(1, half + 1):
        relay(step)
        if chunk < heads:
            send_cot(chunk, 1, n_dp, me, 1)
            chunk += 1
        project_step(step - 1)
        until = blocks * step // half if half > 1 else blocks
        for b in range(turned_blocks, until):
            turn_block(b)
        turned_blocks = until
    for g in range(chunk, heads):
        send_cot(g, 1, n_dp, me, 1)
    turn_own.start()
    turn_twin.start()
    project_step(half)

    def spread(shape, axis):
        token = lax.broadcasted_iota(jnp.int32, shape, axis)
        doc = jnp.zeros(shape, jnp.int32)
        start = jnp.zeros(shape, jnp.int32)
        end = jnp.int32(0)
        for k in range(docs - 1):
            length = len_ref[0, k]
            end = end + length
            past = token >= end
            doc = doc + jnp.where(past, 1, 0)
            start = start + jnp.where(past, length, 0)
        return token, doc, token - start

    square = (tokens, tokens)
    token0, doc0, pos0 = spread(square, 0)
    token1, doc1, _ = spread(square, 1)
    allowed = (doc0 == doc1) & (token1 <= token0)
    allowed = jnp.concatenate([allowed.astype(jnp.float32)] * group, axis=0) > 0.5
    table = (tokens, HEAD_DIM)
    _, _, place = spread(table, 0)
    lane = lax.broadcasted_iota(jnp.int32, table, 1)
    pair = jnp.where(lane < HEAD_DIM // 2, lane, lane - HEAD_DIM // 2).astype(jnp.float32)
    frequency = jnp.exp(pair * jnp.float32(-2.0 * math.log(THETA) / HEAD_DIM))
    angle = place.astype(jnp.float32) * frequency
    cosine = jnp.cos(angle)
    sine = jnp.sin(angle)
    sine = jnp.where(lane < HEAD_DIM // 2, -sine, sine)
    _, doc_s, pos_s = spread((tokens, docs * SLOT), 0)
    column = lax.broadcasted_iota(jnp.int32, (tokens, docs * SLOT), 1)
    picked = jnp.where(doc_s * SLOT + pos_s == column, 1.0, 0.0).astype(jnp.bfloat16)

    def turn(rows, direction):
        return rows * cosine + direction * pltpu.roll(rows, HEAD_DIM // 2, 1) * sine

    def stack(rows):
        return jnp.concatenate(
            [rows[:, h * HEAD_DIM : (h + 1) * HEAD_DIM] for h in range(group)], axis=0
        )

    for g in range(heads):
        cols = slice(g * HEAD_DIM, (g + 1) * HEAD_DIM)
        keys = turn(proj_ref[:, cols], 1.0).astype(jnp.bfloat16)
        key_ref[g] = keys
        val_ref[g] = proj_ref[:, kv_cols + g * HEAD_DIM : kv_cols + (g + 1) * HEAD_DIM].astype(
            jnp.bfloat16
        )
        queries = stack(q_ref[:, g * width : (g + 1) * width])
        scores = jnp.where(allowed, dot(queries, keys, ACROSS) * factor, -1e30)
        expo = jnp.exp(scores - jnp.max(scores, axis=-1, keepdims=True))
        prob_ref[g] = expo / jnp.sum(expo, axis=-1, keepdims=True)

    def peer1(kind, index):
        return at(me + (index - x) * CORES, z) if kind == 0 else at(
            me + (index - y) * CORES * x_size, z
        )

    def peer2(kind, index):
        return peer1(1 - kind, index)

    count1 = (x_size, y_size)
    count2 = (y_size, x_size)
    mine1 = (x, y)
    mine2 = (y, x)

    def start1(g):
        for kind in range(2):
            for s in range(1, count1[kind]):
                to = lax.rem(mine1[kind] + s, count1[kind])
                remote(
                    s1_ref[kind].at[g, to],
                    r1_ref[kind].at[g, mine1[kind]],
                    send1.at[g, kind],
                    recv1.at[g, kind],
                    peer1(kind, to),
                ).start()

    def all1(g, kind):
        some = r1_ref[kind].at[g, pl.ds(0, count1[kind] - 1)]
        return remote(some, some, send1.at[g, kind], recv1.at[g, kind], at(twin, z))

    def start2(g):
        for kind in range(2):
            all1(g, kind).wait_recv()
            own = mine1[kind]
            total = s1_ref[kind][g, own].astype(jnp.float32)
            for s in range(1, count1[kind]):
                total += r1_ref[kind][g, lax.rem(own + s, count1[kind])].astype(jnp.float32)
            s2_ref[kind][g] = total.astype(jnp.bfloat16)
            for s in range(1, count2[kind]):
                to = lax.rem(mine2[kind] + s, count2[kind])
                remote(
                    s2_ref[kind].at[g, to],
                    r2_ref[kind].at[g, mine2[kind]],
                    send2.at[g, kind],
                    recv2.at[g, kind],
                    peer2(kind, to),
                ).start()

    def all2(g, kind):
        some = r2_ref[kind].at[g, pl.ds(0, count2[kind] - 1)]
        return remote(some, some, send2.at[g, kind], recv2.at[g, kind], at(twin, z))

    def start3(g):
        for kind in range(2):
            all2(g, kind).wait_recv()
            own = mine2[kind]
            total = s2_ref[kind][g, own].astype(jnp.float32)
            for s in range(1, count2[kind]):
                total += r2_ref[kind][g, lax.rem(own + s, count2[kind])].astype(jnp.float32)
            s3_ref[g, :, :, kind * HEAD_DIM : (kind + 1) * HEAD_DIM] = total.reshape(
                z_size, block // z_size, HEAD_DIM
            )
        for s in range(1, z_size):
            to = lax.rem(z + s, z_size)
            remote(
                s3_ref.at[g, to], r3_ref.at[g, z], send3.at[g], recv3.at[g], at(me, to)
            ).start()

    def all3(g):
        some = r3_ref.at[g, pl.ds(0, z_size - 1)]
        return remote(some, some, send3.at[g], recv3.at[g], at(twin, z))

    def finish(g):
        all3(g).wait_recv()
        total = s3_ref[g, z]
        for s in range(1, z_size):
            total += r3_ref[g, lax.rem(z + s, z_size)]
        total = total * jnp.float32((tokens * n_dp * z_size) ** (-0.5))
        dkw_ref[:, g * HEAD_DIM : (g + 1) * HEAD_DIM] = total[:, :HEAD_DIM]
        dvw_ref[:, g * HEAD_DIM : (g + 1) * HEAD_DIM] = total[:, HEAD_DIM:]

    def all_cot(g):
        some = cot_refs[g].at[pl.ds(0, n_dp - 1)]
        return remote(some, some, cot_send.at[g], cot_recv.at[g], at(twin, z))

    def grad_copy(g):
        return remote(
            grad_ref.at[g, pl.ds(0, tokens)],
            grad_ref.at[g, pl.ds(tokens, tokens)],
            grad_send.at[g],
            grad_recv.at[g],
            at(twin, z),
        )

    outs = []
    for g in range(heads):
        own_cot[g].wait()
        all_cot(g).wait_recv()
        slots = jnp.concatenate(
            [
                cot_refs[g][rank_ref[0, k]].astype(jnp.float32).reshape(SLOT, width)
                for k in range(docs)
            ],
            axis=0,
        ).astype(jnp.bfloat16)
        grads = stack(dot(picked, slots).astype(jnp.bfloat16))
        queries = stack(q_ref[:, g * width : (g + 1) * width])
        probs = prob_ref[g]
        d_probs = dot(grads, val_ref[g], ACROSS)
        centre = jnp.sum(probs * d_probs, axis=-1, keepdims=True)
        d_scores = (probs * (d_probs - centre)).astype(jnp.bfloat16)
        d_keys = (dot(d_scores, queries, DOWN) * factor).astype(jnp.bfloat16)
        d_values = dot(probs.astype(jnp.bfloat16), grads, DOWN).astype(jnp.bfloat16)
        d_key_pre = turn(d_keys.astype(jnp.float32), -1.0).astype(jnp.bfloat16)
        grad_ref[g, :tokens, :HEAD_DIM] = d_key_pre
        grad_ref[g, :tokens, HEAD_DIM:] = d_values
        grad_copy(g).start()
        d_queries = (dot(d_scores, key_ref[g]) * factor).astype(jnp.bfloat16)
        for h in range(group):
            dq_ref[:, g * width + h * HEAD_DIM : g * width + (h + 1) * HEAD_DIM] = d_queries[
                h * tokens : (h + 1) * tokens
            ]
        cols = pl.ds(g * width, width)
        out = pltpu.make_async_copy(dq_ref.at[:, cols], dq_any.at[:, cols], out_sem.at[g])
        out.start()
        outs.append(out)
        if g >= 1:
            start2(g - 1)
        if g >= 2:
            start3(g - 2)
        if g == 0:
            turn_own.wait()
            turn_twin.wait_recv()
        grad_copy(g).wait_recv()
        partial = dot(pair_ref[...], grad_ref[g]).astype(jnp.bfloat16)
        for b in range(blocks):
            by, bx = b // x_size, b % x_size
            rows = partial[b * block : (b + 1) * block]
            s1_ref[0][g, bx, by] = rows[:, :HEAD_DIM]
            s1_ref[1][g, by, bx] = rows[:, HEAD_DIM:]
        start1(g)

    keys_side = jnp.concatenate([grad_ref[g, :tokens, :HEAD_DIM] for g in range(heads)], axis=1)
    values_side = jnp.concatenate([grad_ref[g, :tokens, HEAD_DIM:] for g in range(heads)], axis=1)
    for j in range(z_size):
        rows = dot(keys_side, w_ref[j, 0], ACROSS) + dot(values_side, w_ref[j, 1], ACROSS)
        di_ref[:, j * shard_rows : (j + 1) * shard_rows] = rows.astype(jnp.bfloat16)
    outs.append(pltpu.make_async_copy(di_ref, di_any, out_sem.at[heads]))
    outs[-1].start()

    last = heads - 1
    start2(last)
    if heads >= 2:
        start3(last - 1)
    start3(last)
    for g in range(heads):
        finish(g)
    outs.append(pltpu.make_async_copy(dkw_ref, dkw_any, out_sem.at[heads + 1]))
    outs.append(pltpu.make_async_copy(dvw_ref, dvw_any, out_sem.at[heads + 2]))
    outs[-2].start()
    outs[-1].start()

    for step in range(1, half + 1):
        for way in range(2):
            for k in pieces(way, step):
                ring_hop(way, step, k).wait_send()
                twin_copy(way, step, k, core).wait_send()
    turn_twin.wait_send()
    for g in range(heads):
        all_cot(g).wait_send()
        grad_copy(g).wait_send()
        all3(g).wait_send()
        for kind in range(2):
            all1(g, kind).wait_send()
            all2(g, kind).wait_send()
    for out in outs:
        out.wait()


def hand_on(count, *refs):
    sem = refs[-1]
    copies = [pltpu.make_async_copy(refs[i], refs[count + i], sem.at[i]) for i in range(count)]
    for copy in copies:
        copy.start()
    for copy in copies:
        copy.wait()


def body(queries, inputs, key_weight, value_weight, lengths, doc_ranks, cotangent):
    n_dp = lax.axis_size("dp")
    z_size = lax.axis_size("fsdp")
    x_size = 4 if n_dp >= 32 else 2
    y_size = n_dp // (CORES * x_size)
    tokens, channels = inputs.shape
    shard_rows, kv_cols = key_weight.shape
    heads = kv_cols // HEAD_DIM
    width = queries.shape[1] // heads
    block = channels // (n_dp)
    own_rows = channels // (n_dp * z_size)
    steps = z_size // 2
    bf16, f32 = jnp.bfloat16, jnp.float32
    any_spec = pl.BlockSpec(memory_space=pl.ANY)
    smem = pl.BlockSpec(memory_space=pltpu.SMEM)
    dma = pltpu.SemaphoreType.DMA

    def entry(*refs):
        refs = list(refs)
        head, cots, rest = refs[:14], refs[14 : 14 + heads], refs[14 + heads :]
        pairs = [rest[11 + 2 * i : 13 + 2 * i] for i in range(4)]
        sizes = (n_dp, y_size, x_size, z_size, heads)
        kernel(sizes, *head, cots, *rest[:11], *pairs, *rest[19:])

    scratch = [
        pltpu.VMEM((tokens, queries.shape[1]), bf16),
        pltpu.VMEM((tokens, channels), bf16),
        pltpu.VMEM((z_size, 2, shard_rows, kv_cols), bf16),
        *[pltpu.VMEM((n_dp, SLOT // SUB, SUB, width), bf16) for _ in range(heads)],
        pltpu.VMEM((tokens, 2 * kv_cols), f32),
        pltpu.VMEM((heads, tokens, HEAD_DIM), bf16),
        pltpu.VMEM((heads, tokens, HEAD_DIM), bf16),
        pltpu.VMEM((heads, tokens * width // HEAD_DIM, tokens), f32),
        pltpu.VMEM((CORES, channels // CORES, tokens), bf16),
        pltpu.VMEM((channels // CORES, CORES * tokens), bf16),
        pltpu.VMEM((heads, CORES * tokens, 2 * HEAD_DIM), bf16),
        pltpu.VMEM(queries.shape, bf16),
        pltpu.VMEM(inputs.shape, bf16),
        pltpu.VMEM((own_rows, kv_cols), f32),
        pltpu.VMEM((own_rows, kv_cols), f32),
        pltpu.VMEM((heads, x_size, y_size, block, HEAD_DIM), bf16),
        pltpu.VMEM((heads, y_size, x_size, block, HEAD_DIM), bf16),
        pltpu.VMEM((heads, x_size, y_size, block, HEAD_DIM), bf16),
        pltpu.VMEM((heads, y_size, x_size, block, HEAD_DIM), bf16),
        pltpu.VMEM((heads, y_size, block, HEAD_DIM), bf16),
        pltpu.VMEM((heads, x_size, block, HEAD_DIM), bf16),
        pltpu.VMEM((heads, y_size, block, HEAD_DIM), bf16),
        pltpu.VMEM((heads, x_size, block, HEAD_DIM), bf16),
        pltpu.VMEM((heads, z_size, own_rows, 2 * HEAD_DIM), f32),
        pltpu.VMEM((heads, z_size, own_rows, 2 * HEAD_DIM), f32),
        dma((4,)),
        dma((heads,)),
        dma((heads,)),
        dma((heads,)),
        dma((2, steps, PIECES)),
        dma((2, steps, PIECES)),
        dma((2, steps, PIECES)),
        dma((2, steps, PIECES)),
        dma((3,)),
        dma((heads,)),
        dma((heads,)),
        dma((heads, 2)),
        dma((heads, 2)),
        dma((heads, 2)),
        dma((heads, 2)),
        dma((heads,)),
        dma((heads,)),
        pltpu.SemaphoreType.REGULAR((2,)),
        dma((heads + 3,)),
    ]
    flops = 2 * tokens * channels * 2 * kv_cols * 4
    shapes = (
        jax.ShapeDtypeStruct(queries.shape, bf16),
        jax.ShapeDtypeStruct(inputs.shape, bf16),
        jax.ShapeDtypeStruct((own_rows, kv_cols), f32),
        jax.ShapeDtypeStruct((own_rows, kv_cols), f32),
    )
    results = pl.pallas_call(
        entry,
        out_shape=shapes,
        in_specs=[any_spec] * 4 + [smem] * 2 + [any_spec],
        out_specs=(any_spec,) * 4,
        scratch_shapes=scratch,
        cost_estimate=pl.CostEstimate(
            flops=flops, bytes_accessed=8 * cotangent.size, transcendentals=0
        ),
        compiler_params=pltpu.CompilerParams(
            collective_id=0, has_side_effects=True, vmem_limit_bytes=60 * 1024 * 1024
        ),
    )(
        queries,
        inputs,
        key_weight,
        value_weight,
        lengths,
        doc_ranks,
        cotangent.reshape(n_dp, SLOT // SUB, SUB, cotangent.shape[1]),
    )
    return pl.pallas_call(
        functools.partial(hand_on, len(shapes)),
        out_shape=shapes,
        in_specs=[any_spec] * len(shapes),
        out_specs=(any_spec,) * len(shapes),
        scratch_shapes=[dma((len(shapes),))],
    )(*results)


def solution(mesh):
    both = P(("dp", "fsdp"), None)
    placed = (both, both, P("fsdp", None), P("fsdp", None), both, both, both)
    return jax.shard_map(
        body, mesh=mesh, in_specs=placed, out_specs=(both,) * 4, check_vma=False
    )
```

```python
import functools
import math

import jax
import jax.numpy as jnp
from jax import lax
from jax.experimental import pallas as pl
from jax.experimental.pallas import tpu as pltpu
from jax.sharding import PartitionSpec as P

HEAD_DIM = 128
SLOT = 24
SUB = 8
PIECES = 4
LAST = 3
CORES = 2
THETA = 500000.0
MESH = pl.DeviceIdType.MESH
ACROSS = (((1,), (1,)), ((), ()))
DOWN = (((0,), (0,)), ((), ()))


def dot(a, b, dims=(((1,), (0,)), ((), ()))):
    return lax.dot_general(a, b, dims, preferred_element_type=jnp.float32)


def kernel(
    sizes,
    q_any,
    in_any,
    kw_any,
    vw_any,
    len_ref,
    rank_ref,
    cot_any,
    dq_any,
    di_any,
    dkw_any,
    dvw_any,
    q_ref,
    in_ref,
    w_ref,
    cot_refs,
    proj_ref,
    key_ref,
    val_ref,
    prob_ref,
    turned_ref,
    pair_ref,
    grad_ref,
    dq_ref,
    di_ref,
    dkw_ref,
    dvw_ref,
    s1_ref,
    r1_ref,
    s2_ref,
    r2_ref,
    s3_ref,
    r3_ref,
    zs_ref,
    zr_ref,
    s4_ref,
    r4_ref,
    load_sem,
    own_sem,
    cot_send,
    cot_recv,
    ring_send,
    ring_recv,
    twin_send,
    twin_recv,
    turn_sem,
    grad_send,
    grad_recv,
    send1,
    recv1,
    send2,
    recv2,
    send3,
    recv3,
    send4,
    recv4,
    zs_sem,
    zr_sem,
    gate,
    out_sem,
):
    n_dp, y_size, x_size, z_size, heads, z_first = sizes
    me = lax.axis_index("dp")
    z = lax.axis_index("fsdp")
    core = lax.rem(me, CORES)
    x = lax.rem(me // CORES, x_size)
    y = me // (CORES * x_size)
    twin = me + 1 - 2 * core
    tokens = q_ref.shape[0]
    width = q_ref.shape[1] // heads
    group = width // HEAD_DIM
    kv_cols = heads * HEAD_DIM
    shard_rows = w_ref.shape[2]
    docs = len_ref.shape[1]
    half = z_size // 2
    factor = HEAD_DIM ** (-0.5)

    right = lax.rem(z + 1, z_size)
    left = lax.rem(z + z_size - 1, z_size)

    def at(dp, fsdp):
        return {"dp": dp, "fsdp": fsdp}

    def at_x(s):
        return me + (lax.rem(x + s, x_size) - x) * CORES

    def at_y(s):
        return me + (lax.rem(y + s, y_size) - y) * CORES * x_size

    def remote(src, dst, send, recv, device):
        return pltpu.make_async_remote_copy(
            src_ref=src,
            dst_ref=dst,
            send_sem=send,
            recv_sem=recv,
            device_id=device,
            device_id_type=MESH,
        )

    loads = [
        pltpu.make_async_copy(kw_any, w_ref.at[z, 0], load_sem.at[0]),
        pltpu.make_async_copy(vw_any, w_ref.at[z, 1], load_sem.at[1]),
        pltpu.make_async_copy(in_any, in_ref, load_sem.at[2]),
        pltpu.make_async_copy(q_any, q_ref, load_sem.at[3]),
    ]
    for load in loads:
        load.start()
    own_cot = [
        pltpu.make_async_copy(
            cot_any.at[me, :, :, pl.ds(g * width, width)], cot_refs[g].at[me], own_sem.at[g]
        )
        for g in range(heads)
    ]

    barrier = pltpu.get_barrier_semaphore()
    around = [(twin, z)] + [(at_y(s), z) for s in range(1, y_size)]
    for s in range(1, x_size):
        around += [(at_x(s), z), (at_x(s) + twin - me, z)]
    around += [(me, to) for to in (right, left)][: z_size - 1]
    for dp, fsdp in around:
        pl.semaphore_signal(barrier, inc=1, device_id=at(dp, fsdp), device_id_type=MESH)
    pl.semaphore_wait(barrier, len(around))

    def pieces(way, step):
        if step < half:
            return list(range(PIECES))
        return list(range(way * PIECES // 2, (way + 1) * PIECES // 2))

    def shard_at(way, step):
        return lax.rem(z + (z_size - step if way == 0 else step), z_size)

    def place_at(way, step, k, kind):
        rows = pl.ds(k * (shard_rows // PIECES), shard_rows // PIECES)
        return w_ref.at[shard_at(way, step), kind, rows]

    def ring_copy(place, way, step, k, device):
        sems = (ring_send.at[way, step - 1, k], ring_recv.at[way, step - 1, k])
        return remote(place, place, *sems, device)

    def ring_hop(way, step, k):
        return ring_copy(
            place_at(way, step - 1, k, core), way, step, k, at(me, right if way == 0 else left)
        )

    def ring_arrival(way, step, k):
        return ring_copy(place_at(way, step, k, core), way, step, k, at(twin, z))

    def twin_copy(way, step, k, kind):
        place = place_at(way, step, k, kind)
        sems = (twin_send.at[way, step - 1, k], twin_recv.at[way, step - 1, k])
        return remote(place, place, *sems, at(twin, z))

    def relay(step):
        for k in range(PIECES):
            for way in range(2):
                if k not in pieces(way, step):
                    continue
                ring_arrival(way, step, k).wait_recv()
                if step < half and k in pieces(way, step + 1):
                    ring_hop(way, step + 1, k).start()
                twin_copy(way, step, k, core).start()

    def from_twin(step):
        for way in range(2):
            for k in pieces(way, step):
                twin_copy(way, step, k, 1 - core).wait_recv()

    loads[0].wait()
    loads[1].wait()
    for k in range(PIECES):
        for way in range(2):
            if k in pieces(way, 1):
                ring_hop(way, 1, k).start()

    for s in range(1, y_size):
        pl.semaphore_signal(gate, inc=1, device_id=at(at_y(s), z), device_id_type=MESH)
    pl.semaphore_wait(gate, y_size - 1)

    def send_cot(g):
        def one(s, carry):
            to = lax.rem(me + s, n_dp)
            remote(
                cot_any.at[to, :, :, pl.ds(g * width, width)],
                cot_refs[g].at[me],
                cot_send.at[g],
                cot_recv.at[g],
                at(to, z),
            ).start()
            return carry

        lax.fori_loop(1, n_dp, one, 0)

    send_cot(0)
    for g in range(heads):
        own_cot[g].start()

    loads[2].wait()
    loads[3].wait()

    def project(shard, first=False):
        cols = pl.ds(pl.multiple_of(shard * shard_rows, shard_rows), shard_rows)
        rows = in_ref[:, cols]
        for kind in range(2):
            out = slice(kind * kv_cols, (kind + 1) * kv_cols)
            term = dot(rows, w_ref[shard, kind])
            if first:
                proj_ref[:, out] = term
            else:
                proj_ref[:, out] += term

    def project_step(step):
        if step == 0:
            project(z, True)
            return
        from_twin(step)
        for way in range(2 if step < half else 1):
            project(shard_at(way, step))

    blocks = y_size * x_size
    block = in_ref.shape[1] // (blocks * CORES)

    def turn_block(b):
        turned = in_ref[:, b * CORES * block : (b + 1) * CORES * block].astype(jnp.float32).T
        turned = turned.astype(jnp.bfloat16)
        for c in range(CORES):
            turned_ref[c, b * block : (b + 1) * block, :] = turned[c * block : (c + 1) * block]

    turn_own = pltpu.make_async_copy(
        turned_ref.at[core], pair_ref.at[:, pl.ds(0, tokens)], turn_sem.at[0]
    )
    turn_twin = remote(
        turned_ref.at[1 - core],
        pair_ref.at[:, pl.ds(tokens, tokens)],
        turn_sem.at[1],
        turn_sem.at[2],
        at(twin, z),
    )

    chunk, turned_blocks = 1, 0
    for step in range(1, half + 1):
        relay(step)
        if chunk < heads:
            send_cot(chunk)
            chunk += 1
        project_step(step - 1)
        until = blocks * step // half if half > 1 else blocks
        for b in range(turned_blocks, until):
            turn_block(b)
        turned_blocks = until
    for g in range(chunk, heads):
        send_cot(g)
    turn_own.start()
    turn_twin.start()
    project_step(half)

    def spread(shape, axis):
        token = lax.broadcasted_iota(jnp.int32, shape, axis)
        doc = jnp.zeros(shape, jnp.int32)
        start = jnp.zeros(shape, jnp.int32)
        end = jnp.int32(0)
        for k in range(docs - 1):
            length = len_ref[0, k]
            end = end + length
            past = token >= end
            doc = doc + jnp.where(past, 1, 0)
            start = start + jnp.where(past, length, 0)
        return token, doc, token - start

    square = (tokens, tokens)
    token0, doc0, pos0 = spread(square, 0)
    token1, doc1, _ = spread(square, 1)
    allowed = (doc0 == doc1) & (token1 <= token0)
    allowed = jnp.concatenate([allowed.astype(jnp.float32)] * group, axis=0) > 0.5
    table = (tokens, HEAD_DIM)
    _, _, place = spread(table, 0)
    lane = lax.broadcasted_iota(jnp.int32, table, 1)
    pair = jnp.where(lane < HEAD_DIM // 2, lane, lane - HEAD_DIM // 2).astype(jnp.float32)
    frequency = jnp.exp(pair * jnp.float32(-2.0 * math.log(THETA) / HEAD_DIM))
    angle = place.astype(jnp.float32) * frequency
    cosine = jnp.cos(angle)
    sine = jnp.sin(angle)
    sine = jnp.where(lane < HEAD_DIM // 2, -sine, sine)
    _, doc_s, pos_s = spread((tokens, docs * SLOT), 0)
    column = lax.broadcasted_iota(jnp.int32, (tokens, docs * SLOT), 1)
    picked = jnp.where(doc_s * SLOT + pos_s == column, 1.0, 0.0).astype(jnp.bfloat16)

    def turn(rows, direction):
        return rows * cosine + direction * pltpu.roll(rows, HEAD_DIM // 2, 1) * sine

    def stack(rows):
        return jnp.concatenate(
            [rows[:, h * HEAD_DIM : (h + 1) * HEAD_DIM] for h in range(group)], axis=0
        )

    for g in range(heads):
        cols = slice(g * HEAD_DIM, (g + 1) * HEAD_DIM)
        keys = turn(proj_ref[:, cols], 1.0).astype(jnp.bfloat16)
        key_ref[g] = keys
        val_ref[g] = proj_ref[:, kv_cols + g * HEAD_DIM : kv_cols + (g + 1) * HEAD_DIM].astype(
            jnp.bfloat16
        )
        queries = stack(q_ref[:, g * width : (g + 1) * width])
        scores = jnp.where(allowed, dot(queries, keys, ACROSS) * factor, -1e30)
        expo = jnp.exp(scores - jnp.max(scores, axis=-1, keepdims=True))
        prob_ref[g] = expo / jnp.sum(expo, axis=-1, keepdims=True)

    def peer1(kind, s):
        return at(at_x(s) if kind == 0 else at_y(s), z)

    count1 = (x_size, y_size)
    count2 = (y_size, x_size)
    mine1 = (x, y)
    mine2 = (y, x)
    own_rows = block // z_size
    scale = jnp.float32((tokens * n_dp * z_size) ** (-0.5))

    def start1(g, partial):
        i = g - z_first
        for b in range(blocks):
            by, bx = b // x_size, b % x_size
            rows = partial[b * block : (b + 1) * block].astype(jnp.bfloat16)
            s1_ref[0][i, bx, by] = rows[:, :HEAD_DIM]
            s1_ref[1][i, by, bx] = rows[:, HEAD_DIM:]
        for kind in range(2):
            for s in range(1, count1[kind]):
                to = lax.rem(mine1[kind] + s, count1[kind])
                remote(
                    s1_ref[kind].at[i, to],
                    r1_ref[kind].at[i, mine1[kind]],
                    send1.at[i, kind],
                    recv1.at[i, kind],
                    peer1(kind, s),
                ).start()

    def all1(g, kind):
        i = g - z_first
        some = r1_ref[kind].at[i, pl.ds(0, count1[kind] - 1)]
        return remote(some, some, send1.at[i, kind], recv1.at[i, kind], at(twin, z))

    def start2(g):
        i = g - z_first
        for kind in range(2):
            all1(g, kind).wait_recv()
            own = mine1[kind]
            total = s1_ref[kind][i, own].astype(jnp.float32)
            for s in range(1, count1[kind]):
                total += r1_ref[kind][i, lax.rem(own + s, count1[kind])].astype(jnp.float32)
            s2_ref[kind][i] = total.astype(jnp.bfloat16)
            for s in range(1, count2[kind]):
                to = lax.rem(mine2[kind] + s, count2[kind])
                remote(
                    s2_ref[kind].at[i, to],
                    r2_ref[kind].at[i, mine2[kind]],
                    send2.at[i, kind],
                    recv2.at[i, kind],
                    peer1(1 - kind, s),
                ).start()

    def all2(g, kind):
        i = g - z_first
        some = r2_ref[kind].at[i, pl.ds(0, count2[kind] - 1)]
        return remote(some, some, send2.at[i, kind], recv2.at[i, kind], at(twin, z))

    def start3(g):
        i = g - z_first
        for kind in range(2):
            all2(g, kind).wait_recv()
            own = mine2[kind]
            total = s2_ref[kind][i, own].astype(jnp.float32)
            for s in range(1, count2[kind]):
                total += r2_ref[kind][i, lax.rem(own + s, count2[kind])].astype(jnp.float32)
            s3_ref[i, :, :, kind * HEAD_DIM : (kind + 1) * HEAD_DIM] = total.reshape(
                z_size, own_rows, HEAD_DIM
            )
        for s in range(1, z_size):
            to = lax.rem(z + s, z_size)
            remote(
                s3_ref.at[i, to], r3_ref.at[i, z], send3.at[i], recv3.at[i], at(me, to)
            ).start()

    def all3(g):
        i = g - z_first
        some = r3_ref.at[i, pl.ds(0, z_size - 1)]
        return remote(some, some, send3.at[i], recv3.at[i], at(twin, z))

    def give(g, total):
        total = total * scale
        dkw_ref[:, g * HEAD_DIM : (g + 1) * HEAD_DIM] = total[:, :HEAD_DIM]
        dvw_ref[:, g * HEAD_DIM : (g + 1) * HEAD_DIM] = total[:, HEAD_DIM:]

    def finish3(g):
        i = g - z_first
        all3(g).wait_recv()
        total = s3_ref[i, z]
        for s in range(1, z_size):
            total += r3_ref[i, lax.rem(z + s, z_size)]
        give(g, total)

    chunk_rows = blocks * own_rows

    def hop_rows(way, step):
        if step == 1:
            return pl.ds(way * (chunk_rows // 2), chunk_rows // 2)
        return pl.ds(0, chunk_rows)

    def hop_copy(g, way, step):
        ahead = half - step + 1
        goal = lax.rem(z + (ahead if way == 0 else z_size - ahead), z_size)
        rows = hop_rows(way, step)
        return remote(
            zs_ref.at[g, goal, rows],
            zr_ref.at[g, way, step - 1, rows],
            zs_sem.at[g, way, step - 1],
            zr_sem.at[g, way, step - 1],
            at(me, right if way == 0 else left),
        )

    def hop(g, step):
        for way in range(2):
            if step > 1:
                hop_copy(g, way, step - 1).wait_recv()
                ahead = half - step + 1
                goal = lax.rem(z + (ahead if way == 0 else z_size - ahead), z_size)
                rows = hop_rows(way, step - 1)
                total = zs_ref[g, goal, rows].astype(jnp.float32)
                total += zr_ref[g, way, step - 2, rows].astype(jnp.float32)
                zs_ref[g, goal, rows] = total.astype(jnp.bfloat16)
            hop_copy(g, way, step).start()

    def start_ring(g, partial):
        apart = partial.reshape(blocks, z_size, own_rows, 2 * HEAD_DIM)
        for j in range(z_size):
            zs_ref[g, j] = (
                apart[:, j].reshape(chunk_rows, 2 * HEAD_DIM).astype(jnp.bfloat16)
            )
        hop(g, 1)

    place_b = y * x_size + x

    def spread_out(g):
        total = zs_ref[g, z].astype(jnp.float32)
        for way in range(2):
            hop_copy(g, way, half).wait_recv()
            if half > 1:
                total += zr_ref[g, way, half - 1].astype(jnp.float32)
        if half == 1:
            total += zr_last(g)
        s4_ref[g] = total.reshape(blocks, own_rows, 2 * HEAD_DIM)

        def one(s, carry):
            to = lax.rem(place_b + s, blocks)
            remote(
                s4_ref.at[g, to],
                r4_ref.at[g, place_b],
                send4.at[g],
                recv4.at[g],
                at(to * CORES + core, z),
            ).start()
            return carry

        lax.fori_loop(1, blocks, one, 0)

    def zr_last(g):
        lower = zr_ref[g, 0, 0, : chunk_rows // 2].astype(jnp.float32)
        upper = zr_ref[g, 1, 0, chunk_rows // 2 :].astype(jnp.float32)
        return jnp.concatenate([lower, upper], axis=0)

    def all4(g):
        some = r4_ref.at[g, pl.ds(0, blocks - 1)]
        return remote(some, some, send4.at[g], recv4.at[g], at(twin, z))

    def finish4(g):
        all4(g).wait_recv()
        total = s4_ref[g, place_b]
        for s in range(1, blocks):
            total += r4_ref[g, lax.rem(place_b + s, blocks)]
        give(g, total)

    def all_cot(g):
        some = cot_refs[g].at[pl.ds(0, n_dp - 1)]
        return remote(some, some, cot_send.at[g], cot_recv.at[g], at(twin, z))

    def grad_copy(g):
        return remote(
            grad_ref.at[g, pl.ds(0, tokens)],
            grad_ref.at[g, pl.ds(tokens, tokens)],
            grad_send.at[g],
            grad_recv.at[g],
            at(twin, z),
        )

    outs = []

    def backward(g):
        own_cot[g].wait()
        all_cot(g).wait_recv()
        slots = jnp.concatenate(
            [
                cot_refs[g][rank_ref[0, k]].astype(jnp.float32).reshape(SLOT, width)
                for k in range(docs)
            ],
            axis=0,
        ).astype(jnp.bfloat16)
        grads = stack(dot(picked, slots).astype(jnp.bfloat16))
        queries = stack(q_ref[:, g * width : (g + 1) * width])
        probs = prob_ref[g]
        d_probs = dot(grads, val_ref[g], ACROSS)
        centre = jnp.sum(probs * d_probs, axis=-1, keepdims=True)
        d_scores = (probs * (d_probs - centre)).astype(jnp.bfloat16)
        d_keys = (dot(d_scores, queries, DOWN) * factor).astype(jnp.bfloat16)
        d_values = dot(probs.astype(jnp.bfloat16), grads, DOWN).astype(jnp.bfloat16)
        d_key_pre = turn(d_keys.astype(jnp.float32), -1.0).astype(jnp.bfloat16)
        grad_ref[g, :tokens, :HEAD_DIM] = d_key_pre
        grad_ref[g, :tokens, HEAD_DIM:] = d_values
        grad_copy(g).start()
        d_queries = (dot(d_scores, key_ref[g]) * factor).astype(jnp.bfloat16)
        for h in range(group):
            dq_ref[:, g * width + h * HEAD_DIM : g * width + (h + 1) * HEAD_DIM] = d_queries[
                h * tokens : (h + 1) * tokens
            ]
        cols = pl.ds(g * width, width)
        out = pltpu.make_async_copy(dq_ref.at[:, cols], dq_any.at[:, cols], out_sem.at[g])
        out.start()
        outs.append(out)

    def start_sum(g):
        grad_copy(g).wait_recv()
        partial = dot(pair_ref[...], grad_ref[g])
        if g < z_first:
            start_ring(g, partial)
        else:
            start1(g, partial)

    turn_own.wait()
    turn_twin.wait_recv()
    hops = [0] * heads

    def advance():
        for g in range(z_first):
            if 0 < hops[g] < half:
                hops[g] += 1
                hop(g, hops[g])
            elif hops[g] == half:
                hops[g] = half + 1
                spread_out(g)

    def begin(g):
        advance()
        start_sum(g)
        hops[g] = 1

    backward(0)
    for g in range(1, heads):
        backward(g)
        begin(g - 1)
    begin(heads - 1)

    keys_side = jnp.concatenate([grad_ref[g, :tokens, :HEAD_DIM] for g in range(heads)], axis=1)
    values_side = jnp.concatenate([grad_ref[g, :tokens, HEAD_DIM:] for g in range(heads)], axis=1)
    for j in range(z_size):
        rows = dot(keys_side, w_ref[j, 0], ACROSS) + dot(values_side, w_ref[j, 1], ACROSS)
        di_ref[:, j * shard_rows : (j + 1) * shard_rows] = rows.astype(jnp.bfloat16)
    outs.append(pltpu.make_async_copy(di_ref, di_any, out_sem.at[heads]))
    outs[-1].start()

    advance()
    for g in range(z_first, heads):
        start2(g)
    advance()
    for g in range(z_first, heads):
        start3(g)
    while any(hops[g] <= half for g in range(z_first)):
        advance()
    for g in range(z_first):
        finish4(g)
    for g in range(z_first, heads):
        finish3(g)
    outs.append(pltpu.make_async_copy(dkw_ref, dkw_any, out_sem.at[heads + 1]))
    outs.append(pltpu.make_async_copy(dvw_ref, dvw_any, out_sem.at[heads + 2]))
    outs[-2].start()
    outs[-1].start()

    for step in range(1, half + 1):
        for way in range(2):
            for k in pieces(way, step):
                ring_hop(way, step, k).wait_send()
                twin_copy(way, step, k, core).wait_send()
    turn_twin.wait_send()
    for g in range(heads):
        all_cot(g).wait_send()
        grad_copy(g).wait_send()
        if g < z_first:
            all4(g).wait_send()
            for way in range(2):
                for step in range(1, half + 1):
                    hop_copy(g, way, step).wait_send()
        else:
            all3(g).wait_send()
            for kind in range(2):
                all1(g, kind).wait_send()
                all2(g, kind).wait_send()
    for out in outs:
        out.wait()


def hand_on(count, *refs):
    given, returned, held = refs[:count], refs[count : 2 * count], refs[2 * count : 3 * count]
    into, out = refs[3 * count :]
    arrivals = [pltpu.make_async_copy(given[i], held[i], into.at[i]) for i in range(count)]
    departures = [pltpu.make_async_copy(held[i], returned[i], out.at[i]) for i in range(count)]
    for arrival in arrivals:
        arrival.start()
    for arrival, departure in zip(arrivals, departures):
        arrival.wait()
        departure.start()
    for departure in departures:
        departure.wait()


def body(queries, inputs, key_weight, value_weight, lengths, doc_ranks, cotangent):
    n_dp = lax.axis_size("dp")
    z_size = lax.axis_size("fsdp")
    x_size = 4 if n_dp >= 32 else 2
    y_size = n_dp // (CORES * x_size)
    tokens, channels = inputs.shape
    shard_rows, kv_cols = key_weight.shape
    heads = kv_cols // HEAD_DIM
    width = queries.shape[1] // heads
    block = channels // (n_dp)
    own_rows = channels // (n_dp * z_size)
    blocks = y_size * x_size
    steps = z_size // 2
    z_first = heads - LAST
    bf16, f32 = jnp.bfloat16, jnp.float32
    any_spec = pl.BlockSpec(memory_space=pl.ANY)
    smem = pl.BlockSpec(memory_space=pltpu.SMEM)
    dma = pltpu.SemaphoreType.DMA

    def entry(*refs):
        refs = list(refs)
        head, cots, rest = refs[:14], refs[14 : 14 + heads], refs[14 + heads :]
        pairs = [rest[11 + 2 * i : 13 + 2 * i] for i in range(4)]
        sizes = (n_dp, y_size, x_size, z_size, heads, z_first)
        kernel(sizes, *head, cots, *rest[:11], *pairs, *rest[19:])

    scratch = [
        pltpu.VMEM((tokens, queries.shape[1]), bf16),
        pltpu.VMEM((tokens, channels), bf16),
        pltpu.VMEM((z_size, 2, shard_rows, kv_cols), bf16),
        *[pltpu.VMEM((n_dp, SLOT // SUB, SUB, width), bf16) for _ in range(heads)],
        pltpu.VMEM((tokens, 2 * kv_cols), f32),
        pltpu.VMEM((heads, tokens, HEAD_DIM), bf16),
        pltpu.VMEM((heads, tokens, HEAD_DIM), bf16),
        pltpu.VMEM((heads, tokens * width // HEAD_DIM, tokens), f32),
        pltpu.VMEM((CORES, channels // CORES, tokens), bf16),
        pltpu.VMEM((channels // CORES, CORES * tokens), bf16),
        pltpu.VMEM((heads, CORES * tokens, 2 * HEAD_DIM), bf16),
        pltpu.VMEM(queries.shape, bf16),
        pltpu.VMEM(inputs.shape, bf16),
        pltpu.VMEM((own_rows, kv_cols), f32),
        pltpu.VMEM((own_rows, kv_cols), f32),
        pltpu.VMEM((LAST, x_size, y_size, block, HEAD_DIM), bf16),
        pltpu.VMEM((LAST, y_size, x_size, block, HEAD_DIM), bf16),
        pltpu.VMEM((LAST, x_size, y_size, block, HEAD_DIM), bf16),
        pltpu.VMEM((LAST, y_size, x_size, block, HEAD_DIM), bf16),
        pltpu.VMEM((LAST, y_size, block, HEAD_DIM), bf16),
        pltpu.VMEM((LAST, x_size, block, HEAD_DIM), bf16),
        pltpu.VMEM((LAST, y_size, block, HEAD_DIM), bf16),
        pltpu.VMEM((LAST, x_size, block, HEAD_DIM), bf16),
        pltpu.VMEM((LAST, z_size, own_rows, 2 * HEAD_DIM), f32),
        pltpu.VMEM((LAST, z_size, own_rows, 2 * HEAD_DIM), f32),
        pltpu.VMEM((z_first, z_size, blocks * own_rows, 2 * HEAD_DIM), bf16),
        pltpu.VMEM((z_first, 2, steps, blocks * own_rows, 2 * HEAD_DIM), bf16),
        pltpu.VMEM((z_first, blocks, own_rows, 2 * HEAD_DIM), f32),
        pltpu.VMEM((z_first, blocks, own_rows, 2 * HEAD_DIM), f32),
        dma((4,)),
        dma((heads,)),
        dma((heads,)),
        dma((heads,)),
        dma((2, steps, PIECES)),
        dma((2, steps, PIECES)),
        dma((2, steps, PIECES)),
        dma((2, steps, PIECES)),
        dma((3,)),
        dma((heads,)),
        dma((heads,)),
        dma((LAST, 2)),
        dma((LAST, 2)),
        dma((LAST, 2)),
        dma((LAST, 2)),
        dma((LAST,)),
        dma((LAST,)),
        dma((z_first,)),
        dma((z_first,)),
        dma((z_first, 2, steps)),
        dma((z_first, 2, steps)),
        pltpu.SemaphoreType.REGULAR,
        dma((heads + 3,)),
    ]
    flops = 2 * tokens * channels * 2 * kv_cols * 4
    shapes = (
        jax.ShapeDtypeStruct(queries.shape, bf16),
        jax.ShapeDtypeStruct(inputs.shape, bf16),
        jax.ShapeDtypeStruct((own_rows, kv_cols), f32),
        jax.ShapeDtypeStruct((own_rows, kv_cols), f32),
    )
    results = pl.pallas_call(
        entry,
        out_shape=shapes,
        in_specs=[any_spec] * 4 + [smem] * 2 + [any_spec],
        out_specs=(any_spec,) * 4,
        scratch_shapes=scratch,
        cost_estimate=pl.CostEstimate(
            flops=flops, bytes_accessed=8 * cotangent.size, transcendentals=0
        ),
        compiler_params=pltpu.CompilerParams(
            collective_id=0, has_side_effects=True, vmem_limit_bytes=60 * 1024 * 1024
        ),
    )(
        queries,
        inputs,
        key_weight,
        value_weight,
        lengths,
        doc_ranks,
        cotangent.reshape(n_dp, SLOT // SUB, SUB, cotangent.shape[1]),
    )
    return pl.pallas_call(
        functools.partial(hand_on, len(shapes)),
        out_shape=shapes,
        in_specs=[any_spec] * len(shapes),
        out_specs=(any_spec,) * len(shapes),
        scratch_shapes=[pltpu.VMEM(each.shape, each.dtype) for each in shapes]
        + [dma((len(shapes),))] * 2,
    )(*results)


def solution(mesh):
    both = P(("dp", "fsdp"), None)
    placed = (both, both, P("fsdp", None), P("fsdp", None), both, both, both)
    return jax.shard_map(
        body, mesh=mesh, in_specs=placed, out_specs=(both,) * 4, check_vma=False
    )
```

```python
import functools
import math

import jax
import jax.numpy as jnp
from jax import lax
from jax.experimental import pallas as pl
from jax.experimental.pallas import tpu as pltpu
from jax.sharding import PartitionSpec as P

HEAD_DIM = 128
SLOT = 24
SUB = 8
PIECES = 2
LAST = 2
ORDER = (
    "F0", "B0", "F1", "S0", "B1", "F2", "S1", "B2", "A0", "F3", "A1", "S2",
    "B3", "A0", "A1", "S3", "D", "A0", "A1", "A2", "A3", "A0", "A1", "A2",
    "A3",
)
CORES = 2
THETA = 500000.0
MESH = pl.DeviceIdType.MESH
ACROSS = (((1,), (1,)), ((), ()))
DOWN = (((0,), (0,)), ((), ()))


def dot(a, b, dims=(((1,), (0,)), ((), ()))):
    return lax.dot_general(a, b, dims, preferred_element_type=jnp.float32)


def kernel(
    sizes,
    q_any,
    in_any,
    kw_any,
    vw_any,
    len_ref,
    rank_ref,
    cot_any,
    dq_any,
    di_any,
    dkw_any,
    dvw_any,
    q_ref,
    in_ref,
    w_ref,
    cot_refs,
    proj_ref,
    key_ref,
    val_ref,
    prob_ref,
    turned_ref,
    pair_ref,
    grad_ref,
    dq_ref,
    di_ref,
    dkw_ref,
    dvw_ref,
    s1_ref,
    r1_ref,
    s2_ref,
    r2_ref,
    s3_ref,
    r3_ref,
    zs_ref,
    zr_ref,
    s4_ref,
    r4_ref,
    load_sem,
    own_sem,
    cot_send,
    cot_recv,
    ring_send,
    ring_recv,
    twin_send,
    twin_recv,
    turn_sem,
    grad_send,
    grad_recv,
    send1,
    recv1,
    send2,
    recv2,
    send3,
    recv3,
    send4,
    recv4,
    zs_sem,
    zr_sem,
    out_sem,
):
    n_dp, y_size, x_size, z_size, heads, z_first = sizes
    me = lax.axis_index("dp")
    z = lax.axis_index("fsdp")
    core = lax.rem(me, CORES)
    x = lax.rem(me // CORES, x_size)
    y = me // (CORES * x_size)
    twin = me + 1 - 2 * core
    tokens = q_ref.shape[0]
    width = q_ref.shape[1] // heads
    group = width // HEAD_DIM
    kv_cols = heads * HEAD_DIM
    shard_rows = w_ref.shape[2]
    docs = len_ref.shape[1]
    half = z_size // 2
    factor = HEAD_DIM ** (-0.5)

    right = lax.rem(z + 1, z_size)
    left = lax.rem(z + z_size - 1, z_size)

    def at(dp, fsdp):
        return {"dp": dp, "fsdp": fsdp}

    def at_x(s):
        return me + (lax.rem(x + s, x_size) - x) * CORES

    def at_y(s):
        return me + (lax.rem(y + s, y_size) - y) * CORES * x_size

    def remote(src, dst, send, recv, device):
        return pltpu.make_async_remote_copy(
            src_ref=src,
            dst_ref=dst,
            send_sem=send,
            recv_sem=recv,
            device_id=device,
            device_id_type=MESH,
        )

    loads = [
        pltpu.make_async_copy(kw_any, w_ref.at[z, 0], load_sem.at[0]),
        pltpu.make_async_copy(vw_any, w_ref.at[z, 1], load_sem.at[1]),
        pltpu.make_async_copy(in_any, in_ref, load_sem.at[2]),
        pltpu.make_async_copy(q_any, q_ref, load_sem.at[3]),
    ]
    for load in loads:
        load.start()
    own_cot = [
        pltpu.make_async_copy(
            cot_any.at[me, :, :, pl.ds(g * width, width)], cot_refs[g].at[me], own_sem.at[g]
        )
        for g in range(heads)
    ]

    barrier = pltpu.get_barrier_semaphore()
    for to in (right, left)[: z_size - 1]:
        pl.semaphore_signal(barrier, inc=1, device_id=at(me, to), device_id_type=MESH)

    def greet(s, carry):
        to = lax.rem(me + s, n_dp)
        pl.semaphore_signal(barrier, inc=1, device_id=at(to, z), device_id_type=MESH)
        return carry

    lax.fori_loop(1, n_dp, greet, 0)
    pl.semaphore_wait(barrier, n_dp - 1 + min(2, z_size - 1))

    def pieces(way, step):
        if step < half:
            return list(range(PIECES))
        return list(range(way * PIECES // 2, (way + 1) * PIECES // 2))

    def shard_at(way, step):
        return lax.rem(z + (z_size - step if way == 0 else step), z_size)

    def place_at(way, step, k, kind):
        rows = pl.ds(k * (shard_rows // PIECES), shard_rows // PIECES)
        return w_ref.at[shard_at(way, step), kind, rows]

    def ring_copy(place, way, step, k, device):
        sems = (ring_send.at[way, step - 1, k], ring_recv.at[way, step - 1, k])
        return remote(place, place, *sems, device)

    def ring_hop(way, step, k):
        return ring_copy(
            place_at(way, step - 1, k, core), way, step, k, at(me, right if way == 0 else left)
        )

    def ring_arrival(way, step, k):
        return ring_copy(place_at(way, step, k, core), way, step, k, at(twin, z))

    def twin_copy(way, step, k, kind):
        place = place_at(way, step, k, kind)
        sems = (twin_send.at[way, step - 1, k], twin_recv.at[way, step - 1, k])
        return remote(place, place, *sems, at(twin, z))

    def relay(step):
        for k in range(PIECES):
            for way in range(2):
                if k not in pieces(way, step):
                    continue
                ring_arrival(way, step, k).wait_recv()
                if step < half and k in pieces(way, step + 1):
                    ring_hop(way, step + 1, k).start()
                twin_copy(way, step, k, core).start()

    def from_twin(step):
        for way in range(2):
            for k in pieces(way, step):
                twin_copy(way, step, k, 1 - core).wait_recv()

    loads[0].wait()
    loads[1].wait()
    for k in range(PIECES):
        for way in range(2):
            if k in pieces(way, 1):
                ring_hop(way, 1, k).start()

    def send_cot(g):
        def one(s, carry):
            to = lax.rem(me + s, n_dp)
            remote(
                cot_any.at[to, :, :, pl.ds(g * width, width)],
                cot_refs[g].at[me],
                cot_send.at[g],
                cot_recv.at[g],
                at(to, z),
            ).start()
            return carry

        lax.fori_loop(1, n_dp, one, 0)

    send_cot(0)
    for g in range(heads):
        own_cot[g].start()

    loads[2].wait()
    loads[3].wait()

    def project(shard, first=False):
        cols = pl.ds(pl.multiple_of(shard * shard_rows, shard_rows), shard_rows)
        rows = in_ref[:, cols]
        for kind in range(2):
            out = slice(kind * kv_cols, (kind + 1) * kv_cols)
            term = dot(rows, w_ref[shard, kind])
            if first:
                proj_ref[:, out] = term
            else:
                proj_ref[:, out] += term

    def project_step(step):
        if step == 0:
            project(z, True)
            return
        from_twin(step)
        for way in range(2 if step < half else 1):
            project(shard_at(way, step))

    blocks = y_size * x_size
    block = in_ref.shape[1] // (blocks * CORES)

    def turn_block(b):
        turned = in_ref[:, b * CORES * block : (b + 1) * CORES * block].astype(jnp.float32).T
        turned = turned.astype(jnp.bfloat16)
        for c in range(CORES):
            turned_ref[c, b * block : (b + 1) * block, :] = turned[c * block : (c + 1) * block]

    turn_own = pltpu.make_async_copy(
        turned_ref.at[core], pair_ref.at[:, pl.ds(0, tokens)], turn_sem.at[0]
    )
    turn_twin = remote(
        turned_ref.at[1 - core],
        pair_ref.at[:, pl.ds(tokens, tokens)],
        turn_sem.at[1],
        turn_sem.at[2],
        at(twin, z),
    )

    def spread(shape, axis):
        token = lax.broadcasted_iota(jnp.int32, shape, axis)
        doc = jnp.zeros(shape, jnp.int32)
        start = jnp.zeros(shape, jnp.int32)
        end = jnp.int32(0)
        for k in range(docs - 1):
            length = len_ref[0, k]
            end = end + length
            past = token >= end
            doc = doc + jnp.where(past, 1, 0)
            start = start + jnp.where(past, length, 0)
        return token, doc, token - start

    square = (tokens, tokens)
    token0, doc0, pos0 = spread(square, 0)
    token1, doc1, _ = spread(square, 1)
    allowed = (doc0 == doc1) & (token1 <= token0)
    allowed = jnp.concatenate([allowed.astype(jnp.float32)] * group, axis=0) > 0.5
    table = (tokens, HEAD_DIM)
    _, _, place = spread(table, 0)
    lane = lax.broadcasted_iota(jnp.int32, table, 1)
    pair = jnp.where(lane < HEAD_DIM // 2, lane, lane - HEAD_DIM // 2).astype(jnp.float32)
    frequency = jnp.exp(pair * jnp.float32(-2.0 * math.log(THETA) / HEAD_DIM))
    angle = place.astype(jnp.float32) * frequency
    cosine = jnp.cos(angle)
    sine = jnp.sin(angle)
    sine = jnp.where(lane < HEAD_DIM // 2, -sine, sine)
    _, doc_s, pos_s = spread((tokens, docs * SLOT), 0)
    column = lax.broadcasted_iota(jnp.int32, (tokens, docs * SLOT), 1)
    picked = jnp.where(doc_s * SLOT + pos_s == column, 1.0, 0.0).astype(jnp.bfloat16)

    def turn(rows, direction):
        return rows * cosine + direction * pltpu.roll(rows, HEAD_DIM // 2, 1) * sine

    def stack(rows):
        return jnp.concatenate(
            [rows[:, h * HEAD_DIM : (h + 1) * HEAD_DIM] for h in range(group)], axis=0
        )

    chunk, turned_blocks = 1, 0
    for step in range(1, half + 1):
        relay(step)
        if chunk < heads:
            send_cot(chunk)
            chunk += 1
        project_step(step - 1)
        until = blocks * step // half if half > 1 else blocks
        for b in range(turned_blocks, until):
            turn_block(b)
        turned_blocks = until
    for g in range(chunk, heads):
        send_cot(g)
    turn_own.start()
    turn_twin.start()
    project_step(half)

    def forward(g):
        cols = slice(g * HEAD_DIM, (g + 1) * HEAD_DIM)
        keys = turn(proj_ref[:, cols], 1.0).astype(jnp.bfloat16)
        key_ref[g] = keys
        val_ref[g] = proj_ref[:, kv_cols + g * HEAD_DIM : kv_cols + (g + 1) * HEAD_DIM].astype(
            jnp.bfloat16
        )
        queries = stack(q_ref[:, g * width : (g + 1) * width])
        scores = jnp.where(allowed, dot(queries, keys, ACROSS) * factor, -1e30)
        expo = jnp.exp(scores - jnp.max(scores, axis=-1, keepdims=True))
        prob_ref[g] = expo / jnp.sum(expo, axis=-1, keepdims=True)

    def peer1(kind, s):
        return at(at_x(s) if kind == 0 else at_y(s), z)

    count1 = (x_size, y_size)
    count2 = (y_size, x_size)
    mine1 = (x, y)
    mine2 = (y, x)
    own_rows = block // z_size
    scale = jnp.float32((tokens * n_dp * z_size) ** (-0.5))

    def start1(g, partial):
        i = g - z_first
        for b in range(blocks):
            by, bx = b // x_size, b % x_size
            rows = partial[b * block : (b + 1) * block].astype(jnp.bfloat16)
            s1_ref[0][i, bx, by] = rows[:, :HEAD_DIM]
            s1_ref[1][i, by, bx] = rows[:, HEAD_DIM:]
        for kind in range(2):
            for s in range(1, count1[kind]):
                to = lax.rem(mine1[kind] + s, count1[kind])
                remote(
                    s1_ref[kind].at[i, to],
                    r1_ref[kind].at[i, mine1[kind]],
                    send1.at[i, kind],
                    recv1.at[i, kind],
                    peer1(kind, s),
                ).start()

    def all1(g, kind):
        i = g - z_first
        some = r1_ref[kind].at[i, pl.ds(0, count1[kind] - 1)]
        return remote(some, some, send1.at[i, kind], recv1.at[i, kind], at(twin, z))

    def start2(g):
        i = g - z_first
        for kind in range(2):
            all1(g, kind).wait_recv()
            own = mine1[kind]
            total = s1_ref[kind][i, own].astype(jnp.float32)
            for s in range(1, count1[kind]):
                total += r1_ref[kind][i, lax.rem(own + s, count1[kind])].astype(jnp.float32)
            s2_ref[kind][i] = total.astype(jnp.bfloat16)
            for s in range(1, count2[kind]):
                to = lax.rem(mine2[kind] + s, count2[kind])
                remote(
                    s2_ref[kind].at[i, to],
                    r2_ref[kind].at[i, mine2[kind]],
                    send2.at[i, kind],
                    recv2.at[i, kind],
                    peer1(1 - kind, s),
                ).start()

    def all2(g, kind):
        i = g - z_first
        some = r2_ref[kind].at[i, pl.ds(0, count2[kind] - 1)]
        return remote(some, some, send2.at[i, kind], recv2.at[i, kind], at(twin, z))

    def start3(g):
        i = g - z_first
        for kind in range(2):
            all2(g, kind).wait_recv()
            own = mine2[kind]
            total = s2_ref[kind][i, own].astype(jnp.float32)
            for s in range(1, count2[kind]):
                total += r2_ref[kind][i, lax.rem(own + s, count2[kind])].astype(jnp.float32)
            s3_ref[i, :, :, kind * HEAD_DIM : (kind + 1) * HEAD_DIM] = total.reshape(
                z_size, own_rows, HEAD_DIM
            )
        for s in range(1, z_size):
            to = lax.rem(z + s, z_size)
            remote(
                s3_ref.at[i, to], r3_ref.at[i, z], send3.at[i], recv3.at[i], at(me, to)
            ).start()

    def all3(g):
        i = g - z_first
        some = r3_ref.at[i, pl.ds(0, z_size - 1)]
        return remote(some, some, send3.at[i], recv3.at[i], at(twin, z))

    def give(g, total):
        total = total * scale
        dkw_ref[:, g * HEAD_DIM : (g + 1) * HEAD_DIM] = total[:, :HEAD_DIM]
        dvw_ref[:, g * HEAD_DIM : (g + 1) * HEAD_DIM] = total[:, HEAD_DIM:]

    def finish3(g):
        i = g - z_first
        all3(g).wait_recv()
        total = s3_ref[i, z]
        for s in range(1, z_size):
            total += r3_ref[i, lax.rem(z + s, z_size)]
        give(g, total)

    chunk_rows = blocks * own_rows

    def hop_rows(way, step):
        if step == 1:
            return pl.ds(way * (chunk_rows // 2), chunk_rows // 2)
        return pl.ds(0, chunk_rows)

    def hop_copy(g, way, step):
        ahead = half - step + 1
        goal = lax.rem(z + (ahead if way == 0 else z_size - ahead), z_size)
        rows = hop_rows(way, step)
        return remote(
            zs_ref.at[g, goal, rows],
            zr_ref.at[g, way, step - 1, rows],
            zs_sem.at[g, way, step - 1],
            zr_sem.at[g, way, step - 1],
            at(me, right if way == 0 else left),
        )

    def hop(g, step):
        for way in range(2):
            if step > 1:
                hop_copy(g, way, step - 1).wait_recv()
                ahead = half - step + 1
                goal = lax.rem(z + (ahead if way == 0 else z_size - ahead), z_size)
                rows = hop_rows(way, step - 1)
                total = zs_ref[g, goal, rows].astype(jnp.float32)
                total += zr_ref[g, way, step - 2, rows].astype(jnp.float32)
                zs_ref[g, goal, rows] = total.astype(jnp.bfloat16)
            hop_copy(g, way, step).start()

    def start_ring(g, partial):
        apart = partial.reshape(blocks, z_size, own_rows, 2 * HEAD_DIM)
        for j in range(z_size):
            zs_ref[g, j] = (
                apart[:, j].reshape(chunk_rows, 2 * HEAD_DIM).astype(jnp.bfloat16)
            )
        hop(g, 1)

    place_b = y * x_size + x

    def spread_out(g):
        total = zs_ref[g, z].astype(jnp.float32)
        for way in range(2):
            hop_copy(g, way, half).wait_recv()
            if half > 1:
                total += zr_ref[g, way, half - 1].astype(jnp.float32)
        if half == 1:
            total += zr_last(g)
        s4_ref[g] = total.reshape(blocks, own_rows, 2 * HEAD_DIM)

        def one(s, carry):
            to = lax.rem(place_b + s, blocks)
            remote(
                s4_ref.at[g, to],
                r4_ref.at[g, place_b],
                send4.at[g],
                recv4.at[g],
                at(to * CORES + core, z),
            ).start()
            return carry

        lax.fori_loop(1, blocks, one, 0)

    def zr_last(g):
        lower = zr_ref[g, 0, 0, : chunk_rows // 2].astype(jnp.float32)
        upper = zr_ref[g, 1, 0, chunk_rows // 2 :].astype(jnp.float32)
        return jnp.concatenate([lower, upper], axis=0)

    def all4(g):
        some = r4_ref.at[g, pl.ds(0, blocks - 1)]
        return remote(some, some, send4.at[g], recv4.at[g], at(twin, z))

    def finish4(g):
        all4(g).wait_recv()
        total = s4_ref[g, place_b]
        for s in range(1, blocks):
            total += r4_ref[g, lax.rem(place_b + s, blocks)]
        give(g, total)

    def all_cot(g):
        some = cot_refs[g].at[pl.ds(0, n_dp - 1)]
        return remote(some, some, cot_send.at[g], cot_recv.at[g], at(twin, z))

    def grad_copy(g):
        return remote(
            grad_ref.at[g, pl.ds(0, tokens)],
            grad_ref.at[g, pl.ds(tokens, tokens)],
            grad_send.at[g],
            grad_recv.at[g],
            at(twin, z),
        )

    outs = []

    def backward(g):
        own_cot[g].wait()
        all_cot(g).wait_recv()
        slots = jnp.concatenate(
            [
                cot_refs[g][rank_ref[0, k]].astype(jnp.float32).reshape(SLOT, width)
                for k in range(docs)
            ],
            axis=0,
        ).astype(jnp.bfloat16)
        grads = stack(dot(picked, slots).astype(jnp.bfloat16))
        queries = stack(q_ref[:, g * width : (g + 1) * width])
        probs = prob_ref[g]
        d_probs = dot(grads, val_ref[g], ACROSS)
        centre = jnp.sum(probs * d_probs, axis=-1, keepdims=True)
        d_scores = (probs * (d_probs - centre)).astype(jnp.bfloat16)
        d_keys = (dot(d_scores, queries, DOWN) * factor).astype(jnp.bfloat16)
        d_values = dot(probs.astype(jnp.bfloat16), grads, DOWN).astype(jnp.bfloat16)
        d_key_pre = turn(d_keys.astype(jnp.float32), -1.0).astype(jnp.bfloat16)
        grad_ref[g, :tokens, :HEAD_DIM] = d_key_pre
        grad_ref[g, :tokens, HEAD_DIM:] = d_values
        grad_copy(g).start()
        d_queries = (dot(d_scores, key_ref[g]) * factor).astype(jnp.bfloat16)
        for h in range(group):
            dq_ref[:, g * width + h * HEAD_DIM : g * width + (h + 1) * HEAD_DIM] = d_queries[
                h * tokens : (h + 1) * tokens
            ]
        cols = pl.ds(g * width, width)
        out = pltpu.make_async_copy(dq_ref.at[:, cols], dq_any.at[:, cols], out_sem.at[g])
        out.start()
        outs.append(out)

    def start_sum(g):
        grad_copy(g).wait_recv()
        partial = dot(pair_ref[...], grad_ref[g])
        if g < z_first:
            start_ring(g, partial)
        else:
            start1(g, partial)

    turn_own.wait()
    turn_twin.wait_recv()

    def inputs_side():
        keys_side = jnp.concatenate([grad_ref[g, :tokens, :HEAD_DIM] for g in range(heads)], axis=1)
        values_side = jnp.concatenate([grad_ref[g, :tokens, HEAD_DIM:] for g in range(heads)], axis=1)
        for j in range(z_size):
            rows = dot(keys_side, w_ref[j, 0], ACROSS) + dot(values_side, w_ref[j, 1], ACROSS)
            di_ref[:, j * shard_rows : (j + 1) * shard_rows] = rows.astype(jnp.bfloat16)
        outs.append(pltpu.make_async_copy(di_ref, di_any, out_sem.at[heads]))
        outs[-1].start()

    pending = {}

    def begin(g):
        start_sum(g)
        if g < z_first:
            pending[g] = [functools.partial(hop, g, step) for step in range(2, half + 1)]
            pending[g] += [functools.partial(spread_out, g), functools.partial(finish4, g)]
        else:
            pending[g] = [functools.partial(each, g) for each in (start2, start3, finish3)]

    def advance(g):
        if pending.get(g):
            pending[g].pop(0)()

    work = {"F": forward, "B": backward, "S": begin, "A": advance}
    for task in ORDER:
        if task == "D":
            inputs_side()
        else:
            work[task[0]](int(task[1]))
    while any(pending.values()):
        for g in range(heads):
            advance(g)
    outs.append(pltpu.make_async_copy(dkw_ref, dkw_any, out_sem.at[heads + 1]))
    outs.append(pltpu.make_async_copy(dvw_ref, dvw_any, out_sem.at[heads + 2]))
    outs[-2].start()
    outs[-1].start()

    for step in range(1, half + 1):
        for way in range(2):
            for k in pieces(way, step):
                ring_hop(way, step, k).wait_send()
                twin_copy(way, step, k, core).wait_send()
    turn_twin.wait_send()
    for g in range(heads):
        all_cot(g).wait_send()
        grad_copy(g).wait_send()
        if g < z_first:
            all4(g).wait_send()
            for way in range(2):
                for step in range(1, half + 1):
                    hop_copy(g, way, step).wait_send()
        else:
            all3(g).wait_send()
            for kind in range(2):
                all1(g, kind).wait_send()
                all2(g, kind).wait_send()
    for out in outs:
        out.wait()


def hand_on(count, *refs):
    given, returned, held = refs[:count], refs[count : 2 * count], refs[2 * count : 3 * count]
    into, out = refs[3 * count :]
    arrivals = [pltpu.make_async_copy(given[i], held[i], into.at[i]) for i in range(count)]
    departures = [pltpu.make_async_copy(held[i], returned[i], out.at[i]) for i in range(count)]
    for arrival in arrivals:
        arrival.start()
    for arrival, departure in zip(arrivals, departures):
        arrival.wait()
        departure.start()
    for departure in departures:
        departure.wait()


def body(queries, inputs, key_weight, value_weight, lengths, doc_ranks, cotangent):
    n_dp = lax.axis_size("dp")
    z_size = lax.axis_size("fsdp")
    x_size = 4 if n_dp >= 32 else 2
    y_size = n_dp // (CORES * x_size)
    tokens, channels = inputs.shape
    shard_rows, kv_cols = key_weight.shape
    heads = kv_cols // HEAD_DIM
    width = queries.shape[1] // heads
    block = channels // (n_dp)
    own_rows = channels // (n_dp * z_size)
    blocks = y_size * x_size
    steps = z_size // 2
    z_first = heads - LAST
    bf16, f32 = jnp.bfloat16, jnp.float32
    any_spec = pl.BlockSpec(memory_space=pl.ANY)
    smem = pl.BlockSpec(memory_space=pltpu.SMEM)
    dma = pltpu.SemaphoreType.DMA

    def entry(*refs):
        refs = list(refs)
        head, cots, rest = refs[:14], refs[14 : 14 + heads], refs[14 + heads :]
        pairs = [rest[11 + 2 * i : 13 + 2 * i] for i in range(4)]
        sizes = (n_dp, y_size, x_size, z_size, heads, z_first)
        kernel(sizes, *head, cots, *rest[:11], *pairs, *rest[19:])

    scratch = [
        pltpu.VMEM((tokens, queries.shape[1]), bf16),
        pltpu.VMEM((tokens, channels), bf16),
        pltpu.VMEM((z_size, 2, shard_rows, kv_cols), bf16),
        *[pltpu.VMEM((n_dp, SLOT // SUB, SUB, width), bf16) for _ in range(heads)],
        pltpu.VMEM((tokens, 2 * kv_cols), f32),
        pltpu.VMEM((heads, tokens, HEAD_DIM), bf16),
        pltpu.VMEM((heads, tokens, HEAD_DIM), bf16),
        pltpu.VMEM((heads, tokens * width // HEAD_DIM, tokens), f32),
        pltpu.VMEM((CORES, channels // CORES, tokens), bf16),
        pltpu.VMEM((channels // CORES, CORES * tokens), bf16),
        pltpu.VMEM((heads, CORES * tokens, 2 * HEAD_DIM), bf16),
        pltpu.VMEM(queries.shape, bf16),
        pltpu.VMEM(inputs.shape, bf16),
        pltpu.VMEM((own_rows, kv_cols), f32),
        pltpu.VMEM((own_rows, kv_cols), f32),
        pltpu.VMEM((LAST, x_size, y_size, block, HEAD_DIM), bf16),
        pltpu.VMEM((LAST, y_size, x_size, block, HEAD_DIM), bf16),
        pltpu.VMEM((LAST, x_size, y_size, block, HEAD_DIM), bf16),
        pltpu.VMEM((LAST, y_size, x_size, block, HEAD_DIM), bf16),
        pltpu.VMEM((LAST, y_size, block, HEAD_DIM), bf16),
        pltpu.VMEM((LAST, x_size, block, HEAD_DIM), bf16),
        pltpu.VMEM((LAST, y_size, block, HEAD_DIM), bf16),
        pltpu.VMEM((LAST, x_size, block, HEAD_DIM), bf16),
        pltpu.VMEM((LAST, z_size, own_rows, 2 * HEAD_DIM), f32),
        pltpu.VMEM((LAST, z_size, own_rows, 2 * HEAD_DIM), f32),
        pltpu.VMEM((z_first, z_size, blocks * own_rows, 2 * HEAD_DIM), bf16),
        pltpu.VMEM((z_first, 2, steps, blocks * own_rows, 2 * HEAD_DIM), bf16),
        pltpu.VMEM((z_first, blocks, own_rows, 2 * HEAD_DIM), f32),
        pltpu.VMEM((z_first, blocks, own_rows, 2 * HEAD_DIM), f32),
        dma((4,)),
        dma((heads,)),
        dma((heads,)),
        dma((heads,)),
        dma((2, steps, PIECES)),
        dma((2, steps, PIECES)),
        dma((2, steps, PIECES)),
        dma((2, steps, PIECES)),
        dma((3,)),
        dma((heads,)),
        dma((heads,)),
        dma((LAST, 2)),
        dma((LAST, 2)),
        dma((LAST, 2)),
        dma((LAST, 2)),
        dma((LAST,)),
        dma((LAST,)),
        dma((z_first,)),
        dma((z_first,)),
        dma((z_first, 2, steps)),
        dma((z_first, 2, steps)),
        dma((heads + 3,)),
    ]
    flops = 2 * tokens * channels * 2 * kv_cols * 4
    shapes = (
        jax.ShapeDtypeStruct(queries.shape, bf16),
        jax.ShapeDtypeStruct(inputs.shape, bf16),
        jax.ShapeDtypeStruct((own_rows, kv_cols), f32),
        jax.ShapeDtypeStruct((own_rows, kv_cols), f32),
    )
    results = pl.pallas_call(
        entry,
        out_shape=shapes,
        in_specs=[any_spec] * 4 + [smem] * 2 + [any_spec],
        out_specs=(any_spec,) * 4,
        scratch_shapes=scratch,
        cost_estimate=pl.CostEstimate(
            flops=flops, bytes_accessed=8 * cotangent.size, transcendentals=0
        ),
        compiler_params=pltpu.CompilerParams(
            collective_id=0, has_side_effects=True, vmem_limit_bytes=60 * 1024 * 1024
        ),
    )(
        queries,
        inputs,
        key_weight,
        value_weight,
        lengths,
        doc_ranks,
        cotangent.reshape(n_dp, SLOT // SUB, SUB, cotangent.shape[1]),
    )
    return pl.pallas_call(
        functools.partial(hand_on, len(shapes)),
        out_shape=shapes,
        in_specs=[any_spec] * len(shapes),
        out_specs=(any_spec,) * len(shapes),
        scratch_shapes=[pltpu.VMEM(each.shape, each.dtype) for each in shapes]
        + [dma((len(shapes),))] * 2,
    )(*results)


def solution(mesh):
    both = P(("dp", "fsdp"), None)
    placed = (both, both, P("fsdp", None), P("fsdp", None), both, both, both)
    return jax.shard_map(
        body, mesh=mesh, in_specs=placed, out_specs=(both,) * 4, check_vma=False
    )
```

```python
import functools
import math

import jax
import jax.numpy as jnp
from jax import lax
from jax.experimental import pallas as pl
from jax.experimental.pallas import tpu as pltpu
from jax.sharding import PartitionSpec as P

HEAD_DIM = 128
SLOT = 24
SUB = 8
PIECES = 2
LAST = 2
ORDER = (
    "F0", "B0", "F1", "S0", "B1", "F2", "S1", "B2", "A0", "F3", "A1", "S2",
    "B3", "A0", "A1", "S3", "D", "A2", "A0", "A1", "A3", "A2", "A3", "A0",
    "A1",
)
CORES = 2
THETA = 500000.0
MESH = pl.DeviceIdType.MESH
ACROSS = (((1,), (1,)), ((), ()))
DOWN = (((0,), (0,)), ((), ()))


def dot(a, b, dims=(((1,), (0,)), ((), ()))):
    return lax.dot_general(a, b, dims, preferred_element_type=jnp.float32)


def kernel(
    sizes,
    q_any,
    in_any,
    kw_any,
    vw_any,
    len_ref,
    rank_ref,
    cot_any,
    dq_any,
    di_any,
    dkw_any,
    dvw_any,
    q_ref,
    in_ref,
    w_ref,
    cot_refs,
    proj_ref,
    key_ref,
    val_ref,
    prob_ref,
    turned_ref,
    pair_ref,
    grad_ref,
    dq_ref,
    di_ref,
    dkw_ref,
    dvw_ref,
    s1_ref,
    r1_ref,
    s2_ref,
    r2_ref,
    s3_ref,
    r3_ref,
    zs_ref,
    zr_ref,
    s4_ref,
    r4_ref,
    load_sem,
    own_sem,
    cot_send,
    cot_recv,
    ring_send,
    ring_recv,
    twin_send,
    twin_recv,
    turn_sem,
    grad_send,
    grad_recv,
    send1,
    recv1,
    send2,
    recv2,
    send3,
    recv3,
    send4,
    recv4,
    zs_sem,
    zr_sem,
    out_sem,
):
    n_dp, y_size, x_size, z_size, heads, z_first = sizes
    me = lax.axis_index("dp")
    z = lax.axis_index("fsdp")
    core = lax.rem(me, CORES)
    x = lax.rem(me // CORES, x_size)
    y = me // (CORES * x_size)
    twin = me + 1 - 2 * core
    tokens = q_ref.shape[0]
    width = q_ref.shape[1] // heads
    group = width // HEAD_DIM
    kv_cols = heads * HEAD_DIM
    shard_rows = w_ref.shape[2]
    docs = len_ref.shape[1]
    half = z_size // 2
    factor = HEAD_DIM ** (-0.5)

    right = lax.rem(z + 1, z_size)
    left = lax.rem(z + z_size - 1, z_size)

    def at(dp, fsdp):
        return {"dp": dp, "fsdp": fsdp}

    def at_x(s):
        return me + (lax.rem(x + s, x_size) - x) * CORES

    def at_y(s):
        return me + (lax.rem(y + s, y_size) - y) * CORES * x_size

    def remote(src, dst, send, recv, device):
        return pltpu.make_async_remote_copy(
            src_ref=src,
            dst_ref=dst,
            send_sem=send,
            recv_sem=recv,
            device_id=device,
            device_id_type=MESH,
        )

    loads = [
        pltpu.make_async_copy(kw_any, w_ref.at[z, 0], load_sem.at[0]),
        pltpu.make_async_copy(vw_any, w_ref.at[z, 1], load_sem.at[1]),
        pltpu.make_async_copy(in_any, in_ref, load_sem.at[2]),
        pltpu.make_async_copy(q_any, q_ref, load_sem.at[3]),
    ]
    for load in loads:
        load.start()
    own_cot = [
        pltpu.make_async_copy(
            cot_any.at[me, :, :, pl.ds(g * width, width)], cot_refs[g].at[me], own_sem.at[g]
        )
        for g in range(heads)
    ]

    barrier = pltpu.get_barrier_semaphore()
    for to in (right, left)[: z_size - 1]:
        pl.semaphore_signal(barrier, inc=1, device_id=at(me, to), device_id_type=MESH)

    def greet(s, carry):
        to = lax.rem(me + s, n_dp)
        pl.semaphore_signal(barrier, inc=1, device_id=at(to, z), device_id_type=MESH)
        return carry

    lax.fori_loop(1, n_dp, greet, 0)
    pl.semaphore_wait(barrier, n_dp - 1 + min(2, z_size - 1))

    def pieces(way, step):
        if step < half:
            return list(range(PIECES))
        return list(range(way * PIECES // 2, (way + 1) * PIECES // 2))

    def shard_at(way, step):
        return lax.rem(z + (z_size - step if way == 0 else step), z_size)

    def place_at(way, step, k, kind):
        rows = pl.ds(k * (shard_rows // PIECES), shard_rows // PIECES)
        return w_ref.at[shard_at(way, step), kind, rows]

    def ring_copy(place, way, step, k, device):
        sems = (ring_send.at[way, step - 1, k], ring_recv.at[way, step - 1, k])
        return remote(place, place, *sems, device)

    def ring_hop(way, step, k):
        return ring_copy(
            place_at(way, step - 1, k, core), way, step, k, at(me, right if way == 0 else left)
        )

    def ring_arrival(way, step, k):
        return ring_copy(place_at(way, step, k, core), way, step, k, at(twin, z))

    def twin_copy(way, step, k, kind):
        place = place_at(way, step, k, kind)
        sems = (twin_send.at[way, step - 1, k], twin_recv.at[way, step - 1, k])
        return remote(place, place, *sems, at(twin, z))

    def relay(step):
        for k in range(PIECES):
            for way in range(2):
                if k not in pieces(way, step):
                    continue
                ring_arrival(way, step, k).wait_recv()
                if step < half and k in pieces(way, step + 1):
                    ring_hop(way, step + 1, k).start()
                twin_copy(way, step, k, core).start()

    def from_twin(step):
        for way in range(2):
            for k in pieces(way, step):
                twin_copy(way, step, k, 1 - core).wait_recv()

    loads[0].wait()
    loads[1].wait()
    for k in range(PIECES):
        for way in range(2):
            if k in pieces(way, 1):
                ring_hop(way, 1, k).start()

    def send_cot(g):
        def one(s, carry):
            to = lax.rem(me + s, n_dp)
            remote(
                cot_any.at[to, :, :, pl.ds(g * width, width)],
                cot_refs[g].at[me],
                cot_send.at[g],
                cot_recv.at[g],
                at(to, z),
            ).start()
            return carry

        lax.fori_loop(1, n_dp, one, 0)

    send_cot(0)
    for g in range(heads):
        own_cot[g].start()

    loads[2].wait()
    loads[3].wait()

    def project(shard, first=False):
        cols = pl.ds(pl.multiple_of(shard * shard_rows, shard_rows), shard_rows)
        rows = in_ref[:, cols]
        for kind in range(2):
            out = slice(kind * kv_cols, (kind + 1) * kv_cols)
            term = dot(rows, w_ref[shard, kind])
            if first:
                proj_ref[:, out] = term
            else:
                proj_ref[:, out] += term

    def project_step(step):
        if step == 0:
            project(z, True)
            return
        from_twin(step)
        for way in range(2 if step < half else 1):
            project(shard_at(way, step))

    blocks = y_size * x_size
    block = in_ref.shape[1] // (blocks * CORES)

    def turn_block(b):
        turned = in_ref[:, b * CORES * block : (b + 1) * CORES * block].astype(jnp.float32).T
        turned = turned.astype(jnp.bfloat16)
        for c in range(CORES):
            turned_ref[c, b * block : (b + 1) * block, :] = turned[c * block : (c + 1) * block]

    turn_own = pltpu.make_async_copy(
        turned_ref.at[core], pair_ref.at[:, pl.ds(0, tokens)], turn_sem.at[0]
    )
    turn_twin = remote(
        turned_ref.at[1 - core],
        pair_ref.at[:, pl.ds(tokens, tokens)],
        turn_sem.at[1],
        turn_sem.at[2],
        at(twin, z),
    )

    def spread(shape, axis):
        token = lax.broadcasted_iota(jnp.int32, shape, axis)
        doc = jnp.zeros(shape, jnp.int32)
        start = jnp.zeros(shape, jnp.int32)
        end = jnp.int32(0)
        for k in range(docs - 1):
            length = len_ref[0, k]
            end = end + length
            past = token >= end
            doc = doc + jnp.where(past, 1, 0)
            start = start + jnp.where(past, length, 0)
        return token, doc, token - start

    square = (tokens, tokens)
    token0, doc0, pos0 = spread(square, 0)
    token1, doc1, _ = spread(square, 1)
    allowed = (doc0 == doc1) & (token1 <= token0)
    allowed = jnp.concatenate([allowed.astype(jnp.float32)] * group, axis=0) > 0.5
    table = (tokens, HEAD_DIM)
    _, _, place = spread(table, 0)
    lane = lax.broadcasted_iota(jnp.int32, table, 1)
    pair = jnp.where(lane < HEAD_DIM // 2, lane, lane - HEAD_DIM // 2).astype(jnp.float32)
    frequency = jnp.exp(pair * jnp.float32(-2.0 * math.log(THETA) / HEAD_DIM))
    angle = place.astype(jnp.float32) * frequency
    cosine = jnp.cos(angle)
    sine = jnp.sin(angle)
    sine = jnp.where(lane < HEAD_DIM // 2, -sine, sine)
    _, doc_s, pos_s = spread((tokens, docs * SLOT), 0)
    column = lax.broadcasted_iota(jnp.int32, (tokens, docs * SLOT), 1)
    picked = jnp.where(doc_s * SLOT + pos_s == column, 1.0, 0.0).astype(jnp.bfloat16)

    def turn(rows, direction):
        return rows * cosine + direction * pltpu.roll(rows, HEAD_DIM // 2, 1) * sine

    def stack(rows):
        return jnp.concatenate(
            [rows[:, h * HEAD_DIM : (h + 1) * HEAD_DIM] for h in range(group)], axis=0
        )

    chunk, turned_blocks = 1, 0
    for step in range(1, half + 1):
        relay(step)
        if chunk < heads:
            send_cot(chunk)
            chunk += 1
        project_step(step - 1)
        until = blocks * step // half if half > 1 else blocks
        for b in range(turned_blocks, until):
            turn_block(b)
        turned_blocks = until
    for g in range(chunk, heads):
        send_cot(g)
    turn_own.start()
    turn_twin.start()
    project_step(half)

    def forward(g):
        cols = slice(g * HEAD_DIM, (g + 1) * HEAD_DIM)
        keys = turn(proj_ref[:, cols], 1.0).astype(jnp.bfloat16)
        key_ref[g] = keys
        val_ref[g] = proj_ref[:, kv_cols + g * HEAD_DIM : kv_cols + (g + 1) * HEAD_DIM].astype(
            jnp.bfloat16
        )
        queries = stack(q_ref[:, g * width : (g + 1) * width])
        scores = jnp.where(allowed, dot(queries, keys, ACROSS) * factor, -1e30)
        expo = jnp.exp(scores - jnp.max(scores, axis=-1, keepdims=True))
        prob_ref[g] = expo / jnp.sum(expo, axis=-1, keepdims=True)

    def peer1(kind, s):
        return at(at_x(s) if kind == 0 else at_y(s), z)

    count1 = (x_size, y_size)
    count2 = (y_size, x_size)
    mine1 = (x, y)
    mine2 = (y, x)
    own_rows = block // z_size
    scale = jnp.float32((tokens * n_dp * z_size) ** (-0.5))

    def start1(g, partial):
        i = g - z_first
        for b in range(blocks):
            by, bx = b // x_size, b % x_size
            rows = partial[b * block : (b + 1) * block].astype(jnp.bfloat16)
            s1_ref[0][i, bx, by] = rows[:, :HEAD_DIM]
            s1_ref[1][i, by, bx] = rows[:, HEAD_DIM:]
        for kind in range(2):
            for s in range(1, count1[kind]):
                to = lax.rem(mine1[kind] + s, count1[kind])
                remote(
                    s1_ref[kind].at[i, to],
                    r1_ref[kind].at[i, mine1[kind]],
                    send1.at[i, kind],
                    recv1.at[i, kind],
                    peer1(kind, s),
                ).start()

    def all1(g, kind):
        i = g - z_first
        some = r1_ref[kind].at[i, pl.ds(0, count1[kind] - 1)]
        return remote(some, some, send1.at[i, kind], recv1.at[i, kind], at(twin, z))

    def start2(g):
        i = g - z_first
        for kind in range(2):
            all1(g, kind).wait_recv()
            own = mine1[kind]
            total = s1_ref[kind][i, own].astype(jnp.float32)
            for s in range(1, count1[kind]):
                total += r1_ref[kind][i, lax.rem(own + s, count1[kind])].astype(jnp.float32)
            s2_ref[kind][i] = total.astype(jnp.bfloat16)
            for s in range(1, count2[kind]):
                to = lax.rem(mine2[kind] + s, count2[kind])
                remote(
                    s2_ref[kind].at[i, to],
                    r2_ref[kind].at[i, mine2[kind]],
                    send2.at[i, kind],
                    recv2.at[i, kind],
                    peer1(1 - kind, s),
                ).start()

    def all2(g, kind):
        i = g - z_first
        some = r2_ref[kind].at[i, pl.ds(0, count2[kind] - 1)]
        return remote(some, some, send2.at[i, kind], recv2.at[i, kind], at(twin, z))

    def start3(g):
        i = g - z_first
        for kind in range(2):
            all2(g, kind).wait_recv()
            own = mine2[kind]
            total = s2_ref[kind][i, own].astype(jnp.float32)
            for s in range(1, count2[kind]):
                total += r2_ref[kind][i, lax.rem(own + s, count2[kind])].astype(jnp.float32)
            s3_ref[i, :, :, kind * HEAD_DIM : (kind + 1) * HEAD_DIM] = total.reshape(
                z_size, own_rows, HEAD_DIM
            )
        for s in range(1, z_size):
            to = lax.rem(z + s, z_size)
            remote(
                s3_ref.at[i, to], r3_ref.at[i, z], send3.at[i], recv3.at[i], at(me, to)
            ).start()

    def all3(g):
        i = g - z_first
        some = r3_ref.at[i, pl.ds(0, z_size - 1)]
        return remote(some, some, send3.at[i], recv3.at[i], at(twin, z))

    def give(g, total):
        total = total * scale
        dkw_ref[:, g * HEAD_DIM : (g + 1) * HEAD_DIM] = total[:, :HEAD_DIM]
        dvw_ref[:, g * HEAD_DIM : (g + 1) * HEAD_DIM] = total[:, HEAD_DIM:]

    def finish3(g):
        i = g - z_first
        all3(g).wait_recv()
        total = s3_ref[i, z]
        for s in range(1, z_size):
            total += r3_ref[i, lax.rem(z + s, z_size)]
        give(g, total)

    chunk_rows = blocks * own_rows

    def hop_rows(way, step):
        if step == 1:
            return pl.ds(way * (chunk_rows // 2), chunk_rows // 2)
        return pl.ds(0, chunk_rows)

    def hop_copy(g, way, step):
        ahead = half - step + 1
        goal = lax.rem(z + (ahead if way == 0 else z_size - ahead), z_size)
        rows = hop_rows(way, step)
        return remote(
            zs_ref.at[g, goal, rows],
            zr_ref.at[g, way, step - 1, rows],
            zs_sem.at[g, way, step - 1],
            zr_sem.at[g, way, step - 1],
            at(me, right if way == 0 else left),
        )

    def hop(g, step):
        for way in range(2):
            if step > 1:
                hop_copy(g, way, step - 1).wait_recv()
                ahead = half - step + 1
                goal = lax.rem(z + (ahead if way == 0 else z_size - ahead), z_size)
                rows = hop_rows(way, step - 1)
                total = zs_ref[g, goal, rows].astype(jnp.float32)
                total += zr_ref[g, way, step - 2, rows].astype(jnp.float32)
                zs_ref[g, goal, rows] = total.astype(jnp.bfloat16)
            hop_copy(g, way, step).start()

    def start_ring(g, partial):
        apart = partial.reshape(blocks, z_size, own_rows, 2 * HEAD_DIM)
        for j in range(z_size):
            zs_ref[g, j] = (
                apart[:, j].reshape(chunk_rows, 2 * HEAD_DIM).astype(jnp.bfloat16)
            )
        hop(g, 1)

    place_b = y * x_size + x

    def spread_out(g):
        total = zs_ref[g, z].astype(jnp.float32)
        for way in range(2):
            hop_copy(g, way, half).wait_recv()
            if half > 1:
                total += zr_ref[g, way, half - 1].astype(jnp.float32)
        if half == 1:
            total += zr_last(g)
        s4_ref[g] = total.reshape(blocks, own_rows, 2 * HEAD_DIM)

        def one(s, carry):
            to = lax.rem(place_b + s, blocks)
            remote(
                s4_ref.at[g, to],
                r4_ref.at[g, place_b],
                send4.at[g],
                recv4.at[g],
                at(to * CORES + core, z),
            ).start()
            return carry

        lax.fori_loop(1, blocks, one, 0)

    def zr_last(g):
        lower = zr_ref[g, 0, 0, : chunk_rows // 2].astype(jnp.float32)
        upper = zr_ref[g, 1, 0, chunk_rows // 2 :].astype(jnp.float32)
        return jnp.concatenate([lower, upper], axis=0)

    def all4(g):
        some = r4_ref.at[g, pl.ds(0, blocks - 1)]
        return remote(some, some, send4.at[g], recv4.at[g], at(twin, z))

    def finish4(g):
        all4(g).wait_recv()
        total = s4_ref[g, place_b]
        for s in range(1, blocks):
            total += r4_ref[g, lax.rem(place_b + s, blocks)]
        give(g, total)

    def all_cot(g):
        some = cot_refs[g].at[pl.ds(0, n_dp - 1)]
        return remote(some, some, cot_send.at[g], cot_recv.at[g], at(twin, z))

    def grad_copy(g):
        return remote(
            grad_ref.at[g, pl.ds(0, tokens)],
            grad_ref.at[g, pl.ds(tokens, tokens)],
            grad_send.at[g],
            grad_recv.at[g],
            at(twin, z),
        )

    outs = []

    def backward(g):
        own_cot[g].wait()
        all_cot(g).wait_recv()
        slots = jnp.concatenate(
            [
                cot_refs[g][rank_ref[0, k]].astype(jnp.float32).reshape(SLOT, width)
                for k in range(docs)
            ],
            axis=0,
        ).astype(jnp.bfloat16)
        grads = stack(dot(picked, slots).astype(jnp.bfloat16))
        queries = stack(q_ref[:, g * width : (g + 1) * width])
        probs = prob_ref[g]
        d_probs = dot(grads, val_ref[g], ACROSS)
        centre = jnp.sum(probs * d_probs, axis=-1, keepdims=True)
        d_scores = (probs * (d_probs - centre)).astype(jnp.bfloat16)
        d_keys = (dot(d_scores, queries, DOWN) * factor).astype(jnp.bfloat16)
        d_values = dot(probs.astype(jnp.bfloat16), grads, DOWN).astype(jnp.bfloat16)
        d_key_pre = turn(d_keys.astype(jnp.float32), -1.0).astype(jnp.bfloat16)
        grad_ref[g, :tokens, :HEAD_DIM] = d_key_pre
        grad_ref[g, :tokens, HEAD_DIM:] = d_values
        grad_copy(g).start()
        d_queries = (dot(d_scores, key_ref[g]) * factor).astype(jnp.bfloat16)
        for h in range(group):
            dq_ref[:, g * width + h * HEAD_DIM : g * width + (h + 1) * HEAD_DIM] = d_queries[
                h * tokens : (h + 1) * tokens
            ]
        cols = pl.ds(g * width, width)
        out = pltpu.make_async_copy(dq_ref.at[:, cols], dq_any.at[:, cols], out_sem.at[g])
        out.start()
        outs.append(out)

    def start_sum(g):
        if g < z_first:
            grad_copy(g).wait_recv()
            partial = dot(pair_ref[...], grad_ref[g])
        else:
            partial = dot(pair_ref[:, :tokens], grad_ref[g, :tokens])
            grad_copy(g).wait_recv()
            partial += dot(pair_ref[:, tokens:], grad_ref[g, tokens:])
        if g < z_first:
            start_ring(g, partial)
        else:
            start1(g, partial)

    turn_own.wait()
    turn_twin.wait_recv()

    def inputs_side():
        keys_side = jnp.concatenate([grad_ref[g, :tokens, :HEAD_DIM] for g in range(heads)], axis=1)
        values_side = jnp.concatenate([grad_ref[g, :tokens, HEAD_DIM:] for g in range(heads)], axis=1)
        for j in range(z_size):
            rows = dot(keys_side, w_ref[j, 0], ACROSS) + dot(values_side, w_ref[j, 1], ACROSS)
            di_ref[:, j * shard_rows : (j + 1) * shard_rows] = rows.astype(jnp.bfloat16)
        outs.append(pltpu.make_async_copy(di_ref, di_any, out_sem.at[heads]))
        outs[-1].start()

    pending = {}

    def begin(g):
        start_sum(g)
        if g < z_first:
            pending[g] = [functools.partial(hop, g, step) for step in range(2, half + 1)]
            pending[g] += [functools.partial(spread_out, g), functools.partial(finish4, g)]
        else:
            pending[g] = [functools.partial(each, g) for each in (start2, start3, finish3)]

    def advance(g):
        if pending.get(g):
            pending[g].pop(0)()

    work = {"F": forward, "B": backward, "S": begin, "A": advance}
    for task in ORDER:
        if task == "D":
            inputs_side()
        else:
            work[task[0]](int(task[1]))
    while any(pending.values()):
        for g in range(heads):
            advance(g)
    outs.append(pltpu.make_async_copy(dkw_ref, dkw_any, out_sem.at[heads + 1]))
    outs.append(pltpu.make_async_copy(dvw_ref, dvw_any, out_sem.at[heads + 2]))
    outs[-2].start()
    outs[-1].start()

    for step in range(1, half + 1):
        for way in range(2):
            for k in pieces(way, step):
                ring_hop(way, step, k).wait_send()
                twin_copy(way, step, k, core).wait_send()
    turn_twin.wait_send()
    for g in range(heads):
        all_cot(g).wait_send()
        grad_copy(g).wait_send()
        if g < z_first:
            all4(g).wait_send()
            for way in range(2):
                for step in range(1, half + 1):
                    hop_copy(g, way, step).wait_send()
        else:
            all3(g).wait_send()
            for kind in range(2):
                all1(g, kind).wait_send()
                all2(g, kind).wait_send()
    for out in outs:
        out.wait()


def hand_on(count, *refs):
    given, returned, held = refs[:count], refs[count : 2 * count], refs[2 * count : 3 * count]
    into, out = refs[3 * count :]
    arrivals = [pltpu.make_async_copy(given[i], held[i], into.at[i]) for i in range(count)]
    departures = [pltpu.make_async_copy(held[i], returned[i], out.at[i]) for i in range(count)]
    for arrival in arrivals:
        arrival.start()
    for arrival, departure in zip(arrivals, departures):
        arrival.wait()
        departure.start()
    for departure in departures:
        departure.wait()


def body(queries, inputs, key_weight, value_weight, lengths, doc_ranks, cotangent):
    n_dp = lax.axis_size("dp")
    z_size = lax.axis_size("fsdp")
    x_size = 4 if n_dp >= 32 else 2
    y_size = n_dp // (CORES * x_size)
    tokens, channels = inputs.shape
    shard_rows, kv_cols = key_weight.shape
    heads = kv_cols // HEAD_DIM
    width = queries.shape[1] // heads
    block = channels // (n_dp)
    own_rows = channels // (n_dp * z_size)
    blocks = y_size * x_size
    steps = z_size // 2
    z_first = heads - LAST
    bf16, f32 = jnp.bfloat16, jnp.float32
    any_spec = pl.BlockSpec(memory_space=pl.ANY)
    smem = pl.BlockSpec(memory_space=pltpu.SMEM)
    dma = pltpu.SemaphoreType.DMA

    def entry(*refs):
        refs = list(refs)
        head, cots, rest = refs[:14], refs[14 : 14 + heads], refs[14 + heads :]
        pairs = [rest[11 + 2 * i : 13 + 2 * i] for i in range(4)]
        sizes = (n_dp, y_size, x_size, z_size, heads, z_first)
        kernel(sizes, *head, cots, *rest[:11], *pairs, *rest[19:])

    scratch = [
        pltpu.VMEM((tokens, queries.shape[1]), bf16),
        pltpu.VMEM((tokens, channels), bf16),
        pltpu.VMEM((z_size, 2, shard_rows, kv_cols), bf16),
        *[pltpu.VMEM((n_dp, SLOT // SUB, SUB, width), bf16) for _ in range(heads)],
        pltpu.VMEM((tokens, 2 * kv_cols), f32),
        pltpu.VMEM((heads, tokens, HEAD_DIM), bf16),
        pltpu.VMEM((heads, tokens, HEAD_DIM), bf16),
        pltpu.VMEM((heads, tokens * width // HEAD_DIM, tokens), f32),
        pltpu.VMEM((CORES, channels // CORES, tokens), bf16),
        pltpu.VMEM((channels // CORES, CORES * tokens), bf16),
        pltpu.VMEM((heads, CORES * tokens, 2 * HEAD_DIM), bf16),
        pltpu.VMEM(queries.shape, bf16),
        pltpu.VMEM(inputs.shape, bf16),
        pltpu.VMEM((own_rows, kv_cols), f32),
        pltpu.VMEM((own_rows, kv_cols), f32),
        pltpu.VMEM((LAST, x_size, y_size, block, HEAD_DIM), bf16),
        pltpu.VMEM((LAST, y_size, x_size, block, HEAD_DIM), bf16),
        pltpu.VMEM((LAST, x_size, y_size, block, HEAD_DIM), bf16),
        pltpu.VMEM((LAST, y_size, x_size, block, HEAD_DIM), bf16),
        pltpu.VMEM((LAST, y_size, block, HEAD_DIM), bf16),
        pltpu.VMEM((LAST, x_size, block, HEAD_DIM), bf16),
        pltpu.VMEM((LAST, y_size, block, HEAD_DIM), bf16),
        pltpu.VMEM((LAST, x_size, block, HEAD_DIM), bf16),
        pltpu.VMEM((LAST, z_size, own_rows, 2 * HEAD_DIM), f32),
        pltpu.VMEM((LAST, z_size, own_rows, 2 * HEAD_DIM), f32),
        pltpu.VMEM((z_first, z_size, blocks * own_rows, 2 * HEAD_DIM), bf16),
        pltpu.VMEM((z_first, 2, steps, blocks * own_rows, 2 * HEAD_DIM), bf16),
        pltpu.VMEM((z_first, blocks, own_rows, 2 * HEAD_DIM), f32),
        pltpu.VMEM((z_first, blocks, own_rows, 2 * HEAD_DIM), f32),
        dma((4,)),
        dma((heads,)),
        dma((heads,)),
        dma((heads,)),
        dma((2, steps, PIECES)),
        dma((2, steps, PIECES)),
        dma((2, steps, PIECES)),
        dma((2, steps, PIECES)),
        dma((3,)),
        dma((heads,)),
        dma((heads,)),
        dma((LAST, 2)),
        dma((LAST, 2)),
        dma((LAST, 2)),
        dma((LAST, 2)),
        dma((LAST,)),
        dma((LAST,)),
        dma((z_first,)),
        dma((z_first,)),
        dma((z_first, 2, steps)),
        dma((z_first, 2, steps)),
        dma((heads + 3,)),
    ]
    flops = 2 * tokens * channels * 2 * kv_cols * 4
    shapes = (
        jax.ShapeDtypeStruct(queries.shape, bf16),
        jax.ShapeDtypeStruct(inputs.shape, bf16),
        jax.ShapeDtypeStruct((own_rows, kv_cols), f32),
        jax.ShapeDtypeStruct((own_rows, kv_cols), f32),
    )
    results = pl.pallas_call(
        entry,
        out_shape=shapes,
        in_specs=[any_spec] * 4 + [smem] * 2 + [any_spec],
        out_specs=(any_spec,) * 4,
        scratch_shapes=scratch,
        cost_estimate=pl.CostEstimate(
            flops=flops, bytes_accessed=8 * cotangent.size, transcendentals=0
        ),
        compiler_params=pltpu.CompilerParams(
            collective_id=0, has_side_effects=True, vmem_limit_bytes=60 * 1024 * 1024
        ),
    )(
        queries,
        inputs,
        key_weight,
        value_weight,
        lengths,
        doc_ranks,
        cotangent.reshape(n_dp, SLOT // SUB, SUB, cotangent.shape[1]),
    )
    return pl.pallas_call(
        functools.partial(hand_on, len(shapes)),
        out_shape=shapes,
        in_specs=[any_spec] * len(shapes),
        out_specs=(any_spec,) * len(shapes),
        scratch_shapes=[pltpu.VMEM(each.shape, each.dtype) for each in shapes]
        + [dma((len(shapes),))] * 2,
    )(*results)


def solution(mesh):
    both = P(("dp", "fsdp"), None)
    placed = (both, both, P("fsdp", None), P("fsdp", None), both, both, both)
    return jax.shard_map(
        body, mesh=mesh, in_specs=placed, out_specs=(both,) * 4, check_vma=False
    )
```
